256 devices in a mesh: chan: 32 (over z, y_lo, core), win: 8 (over x, y_hi).
Axes of the slice: x: 4, y: 4 (y_hi: 2, y_lo: 2; y = y_hi * 2 + y_lo), z: 8, core: 2. Of those that a mesh axis runs over, the one named last changes fastest.
Arguments:
- spectra: bfloat16 [16, 2048, 2, 2048], P('win', 'chan'), may hold values from -180 to 180, as said below
- band_offsets: int32 [32, 2], P('chan'), may hold values from -256 to 256, as said below
- window_keep: int32 [16], P('win'), may hold values 0 or 1
- chan_dist: int32 [2048], replicated, may hold values from 0 to 2047, as said below
Outputs:
- linear_stack: float32 [2048, 2, 1024], P('chan')
- phase_stack: float32 [2048, 2, 1024], P('chan')
- distance_gather: float32 [1024, 1024], P('chan')
The draws below stay inside these ranges and needn't reach their ends.
Inputs may be any that keep to these rules, and one draw needn't show every extreme that they name: `spectra`: spectra with row and frequency scales. `band_offsets`: each block's 2 offsets are nonzero; the first and the last block each hold both +256 and -256. `chan_dist`: never falls from one channel to the next, by steps of 0, 1 or 2; the first channel has 0 and the last has 2047.
All inputs are finite; a program needn't handle non-finite values. No bound on the sum of `window_keep` on one device may be relied on, other than what follows from the above.
Results may differ from the reference program's by a relative error of at most 0.015.
Values may be sent and summed in bfloat16 or wider, within the bound.
A program may use at most 64 MiB of HBM per device.

```python
import math
import jax
import jax.numpy as jnp
from jax import lax

F = 2048
LAGS = 1024
CH_DEV = 64
NOFF = 2
HALF = 256
NBIN = 32
WINDOWS = 16
CHANNELS = 2048
N_CHAN = 32


def draw_spectra(key, part):
    k_base, k_rows, k_cols = jax.random.split(key, 3)
    rows = jnp.exp(jax.random.uniform(k_rows, (WINDOWS, CHANNELS, 1, 1), minval=0.0, maxval=math.log(10.0)))
    cols = jnp.exp(jax.random.uniform(k_cols, (1, 1, 1, F), minval=math.log(0.3), maxval=math.log(3.0)))
    base = jnp.clip(jax.random.normal(k_base, (WINDOWS, CHANNELS, 2, F)), -6.0, 6.0)
    return (base * rows * cols).astype(jnp.float32).astype(jnp.bfloat16)


def draw_band_offsets(key, part):
    k_size, k_sign = jax.random.split(jax.random.fold_in(key, 11))
    sizes = jax.random.randint(k_size, (N_CHAN, NOFF), 1, HALF + 1)
    signs = jax.random.randint(k_sign, (N_CHAN, NOFF), 0, 2) * 2 - 1
    values = (sizes * signs).astype(jnp.int32)
    values = values.at[0, 0].set(HALF)
    values = values.at[0, 1].set(-HALF)
    values = values.at[N_CHAN - 1, 0].set(-HALF)
    values = values.at[N_CHAN - 1, 1].set(HALF)
    return values


def draw_chan_dist(key, part):
    jitter = jax.random.randint(jax.random.fold_in(key, 23), (CHANNELS,), 0, 2)
    jitter = jitter.at[0].set(0).at[CHANNELS - 1].set(0)
    return (jnp.arange(CHANNELS, dtype=jnp.int32) + jitter).astype(jnp.int32)


def place_ends(values, stream_key, smallest, high):
    place = [jax.random.randint(jax.random.fold_in(stream_key, axis), (), 0, length) for axis, length in enumerate(values.shape)]
    main_axis = values.shape.index(max(values.shape))
    next_to = place[:main_axis] + [(place[main_axis] + 1) % values.shape[main_axis]] + place[main_axis + 1:]
    return values.at[tuple(place)].set(smallest).at[tuple(next_to)].set(high)


def setup_inputs(seed: int = 0) -> dict:
    streams_of = jax.random.split(jax.random.key(seed), 5)
    return {
        "spectra": draw_spectra(jax.random.fold_in(streams_of[4], 71), 0),
        "band_offsets": draw_band_offsets(jax.random.fold_in(streams_of[4], 71), 0),
        "window_keep": place_ends((jax.random.randint(streams_of[2], (WINDOWS,), 0, 4) < 3).astype(jnp.int32), jax.random.fold_in(streams_of[2], 1), 0, 1),
        "chan_dist": draw_chan_dist(jax.random.fold_in(streams_of[4], 71), 0),
    }


EPS = 1e-06
FLOOR = 0.1

def dft_table(freqs, first_lag, count):
    bins = jnp.arange(freqs, dtype=jnp.int32)[:, None]
    shifts = first_lag + jnp.arange(count, dtype=jnp.int32)[None, :]
    turns = jnp.mod(bins * shifts, 2 * freqs).astype(jnp.float32)
    angle = turns * (math.pi / freqs)
    cosine = jnp.cos(angle) / math.sqrt(freqs)
    sine = jnp.sin(angle) / math.sqrt(freqs)
    upper = jnp.concatenate([cosine, sine], axis=1)
    lower = jnp.concatenate([-sine, cosine], axis=1)
    return jnp.concatenate([upper, lower], axis=0).astype(jnp.bfloat16)

def whiten(spectra):
    values = spectra.astype(jnp.float32)
    power = lax.optimization_barrier(jnp.mean(values[:, :, 0] ** 2 + values[:, :, 1] ** 2, axis=-1))
    return (values * lax.rsqrt(power + EPS)[:, :, None, None]).astype(jnp.bfloat16)

def cross_pair(mine, other):
    mine = mine.astype(jnp.float32)
    other = other.astype(jnp.float32)
    real = mine[..., 0, :] * other[..., 0, :] + mine[..., 1, :] * other[..., 1, :]
    imag = mine[..., 1, :] * other[..., 0, :] - mine[..., 0, :] * other[..., 1, :]
    return jnp.concatenate([real, imag], axis=-1).astype(jnp.bfloat16)

def reference(spectra, band_offsets, window_keep, chan_dist):
    windows, channels, _, freqs = spectra.shape
    n_off = band_offsets.shape[1]
    table = dft_table(freqs, -(LAGS // 2), LAGS)
    index = jnp.arange(channels, dtype=jnp.int32)
    block = (index // CH_DEV).astype(jnp.int32)
    offsets = band_offsets[block]
    partner = jnp.mod(index[:, None] + offsets, channels).astype(jnp.int32)

    def one_window(carry, inputs):
        spec, keep = inputs
        white = whiten(spec[None])[0]
        other = white[partner]
        cross = cross_pair(white[:, None], other).reshape(channels * n_off, 2 * freqs)
        analytic = jnp.dot(cross, table, preferred_element_type=jnp.float32)
        real = analytic[:, :LAGS]
        imag = analytic[:, LAGS:]
        weight = keep.astype(jnp.float32)
        scale = weight / jnp.maximum(jnp.sqrt(real * real + imag * imag), FLOOR)
        lin_sum, re_sum, im_sum = carry
        return ((lin_sum + weight * real, re_sum + scale * real, im_sum + scale * imag), None)
    zeros = jnp.zeros((channels * n_off, LAGS), jnp.float32)
    (lin_sum, re_sum, im_sum), _ = lax.scan(one_window, (zeros, zeros, zeros), (spectra, window_keep))
    linear = lin_sum / math.sqrt(windows)
    phased = linear * jnp.sqrt(re_sum * re_sum + im_sum * im_sum) / windows
    own_dist = chan_dist[:, None]
    partner_dist = chan_dist[partner]
    bins = jnp.minimum(jnp.abs(partner_dist - own_dist), NBIN - 1)
    segment = (block[:, None] * NBIN + bins).astype(jnp.int32).reshape(-1)
    gathered = jax.ops.segment_sum(linear, segment, num_segments=N_CHAN * NBIN)
    return (linear.reshape(channels, n_off, LAGS), phased.reshape(channels, n_off, LAGS), gathered)
```

```python
import functools
import math

import jax
import jax.numpy as jnp
from jax import lax
from jax.experimental import pallas as pl
from jax.experimental.pallas import tpu as pltpu
from jax.sharding import PartitionSpec as P

LAGS = 1024
NBIN = 32
EPS = 1e-06
FLOOR = 0.1

F = 2048
CH = 64
Q = 4
L = F // 128 // Q
KQ = L * 128
FINE = 32
MESH = pl.DeviceIdType.MESH


def whiten(spectra):
    values = spectra.astype(jnp.float32)
    power = jnp.mean(values[:, :, 0] ** 2 + values[:, :, 1] ** 2, axis=-1)
    return (values * lax.rsqrt(power + EPS)[:, :, None, None]).astype(jnp.bfloat16)


def turn(product):
    return jnp.bitwise_and(product, 2 * F - 1).astype(jnp.float32) * (math.pi / F)


def kernel(
    wt, offs, keep, member,
    lin_out, ph_out, bin_out,
    j0, j1, j2, j3, j32, ea, eb, table, x, acc, s,
    ra, rb, pa, pb, ra2, rb2, g,
    local_sem, send_sem, recv_sem,
):
    joined = (j0, j1, j2, j3)
    chan = lax.axis_index("chan")
    win = lax.axis_index("win")
    core = lax.rem(chan, 2)
    ylo = lax.rem(chan // 2, 2)
    xx = win // 2
    yhi = lax.rem(win, 2)
    yy = yhi * 2 + ylo
    base = chan - ylo * 2
    above = lax.rem(chan + 4, 32)
    below = lax.rem(chan + 28, 32)
    mate = chan + 1 - 2 * core
    across = chan + 2 - 4 * ylo
    own = ylo * 2 + core
    far = (1 - ylo) * 2 + core

    x_peer = [lax.rem(xx + d, 4) for d in (1, 2, 3)]
    y_peer = [lax.rem(yy + d, 4) for d in (1, 2, 3)]
    x_dev = [{"chan": chan, "win": p * 2 + yhi} for p in x_peer]
    y_dev = [{"chan": base + lax.rem(p, 2) * 2, "win": xx * 2 + p // 2} for p in y_peer]
    g_dev = [{"chan": chan, "win": win + 1 - 2 * yhi}] + [
        dev for p in x_peer for dev in (
            {"chan": chan, "win": p * 2 + yhi}, {"chan": chan, "win": p * 2 + 1 - yhi})
    ]

    barrier = pltpu.get_barrier_semaphore()
    greet = [{"chan": c, "win": win} for c in (above, below, mate)] + y_dev + x_dev + [
        {"chan": chan, "win": p * 2 + 1 - yhi} for p in x_peer
    ]
    for dev in greet:
        pl.semaphore_signal(barrier, inc=1, device_id=dev, device_id_type=MESH)
    pl.semaphore_wait(barrier, len(greet))

    count = [0]
    sent = []

    def send(src, dst, device):
        i = count[0]
        count[0] += 1
        copy = pltpu.make_async_remote_copy(
            src_ref=src, dst_ref=dst, send_sem=send_sem.at[i], recv_sem=recv_sem.at[i],
            device_id=device, device_id_type=MESH,
        )
        copy.start()
        sent.append(copy)
        return copy

    def near(c):
        return {"chan": c, "win": win}

    lanes = [pl.ds(q * L, L) for q in range(Q)]
    stay, cross_y, up, down, mate_own = [], [], [], [], []
    for q in range(Q):
        mine = wt.at[ylo, lanes[q]]
        copy = pltpu.make_async_copy(mine, joined[q].at[4 + own], local_sem.at[q])
        copy.start()
        stay.append(copy)
        cross_y.append(send(wt.at[1 - ylo, lanes[q]], joined[q].at[4 + own], near(across)))
        up.append(send(mine, joined[q].at[own], near(above)))
        down.append(send(mine, joined[q].at[8 + own], near(below)))
        mate_own.append(send(mine, joined[q].at[4 + own], near(mate)))

    lag = lax.broadcasted_iota(jnp.int32, (FINE, LAGS), 1) - LAGS // 2
    row = lax.broadcasted_iota(jnp.int32, (FINE, LAGS), 0)
    fine = turn(row * lag)
    eb[0] = jnp.cos(fine) * (1.0 / math.sqrt(F))
    eb[1] = jnp.sin(fine) * (1.0 / math.sqrt(F))
    for half in range(F // FINE // FINE):
        coarse = turn((row + half * FINE) * FINE * lag)
        ea[0, half * FINE:(half + 1) * FINE] = jnp.cos(coarse)
        ea[1, half * FINE:(half + 1) * FINE] = jnp.sin(coarse)

    per = KQ // FINE

    def fill(a, _):
        ca = ea[0, pl.ds(a, 1), :]
        sa = ea[1, pl.ds(a, 1), :]
        q2 = (a // per) * 2
        at = pl.ds(pl.multiple_of(lax.rem(a, per) * FINE, FINE), FINE)
        table[q2, at, :] = (eb[0] * ca - eb[1] * sa).astype(jnp.bfloat16)
        table[q2 + 1, at, :] = (eb[1] * ca + eb[0] * sa).astype(jnp.bfloat16)
        return 0

    lax.fori_loop(0, F // FINE, fill, 0)

    up_far, down_far, mate_far = [], [], []
    for q in range(Q):
        cross_y[q].wait_recv()
        mine = joined[q].at[4 + far]
        up_far.append(send(mine, joined[q].at[far], near(above)))
        down_far.append(send(mine, joined[q].at[8 + far], near(below)))
        mate_far.append(send(mine, joined[q].at[4 + far], near(mate)))

    def forward(q):
        for copy in (up[q], down[q], up_far[q], down_far[q]):
            copy.wait_recv()
        return [
            send(joined[q].at[pos], joined[q].at[pos], near(mate))
            for pos in (2 + core, 8 + core, 10 - 9 * core)
        ]

    starts = []
    for b in range(2):
        block = core + 2 * b
        which = jnp.where(block == own, 0, 1)
        for k in range(2):
            starts.append(((4 + block) * CH, (4 + block) * CH + jnp.where(
                block == own, offs[0, k], offs[1, k])))

    for q in range(Q):
        moved = forward(q)
        stay[q].wait()
        mate_own[q].wait_recv()
        mate_far[q].wait_recv()
        for copy in moved:
            copy.wait_recv()

        def widen(i, _):
            p = core + i
            at = pl.ds(pl.multiple_of(p * CH, CH), CH)
            for lg in range(L):
                for ri in range(2):
                    j32[lg * 2 + ri, at, :] = joined[q][p, lg, ri].astype(jnp.float32)
            return 0

        lax.fori_loop(0, 11, widen, 0)
        for r, (mine_at, other_at) in enumerate(starts):
            at_m = pl.ds(pl.multiple_of(mine_at, CH), CH)
            at_o = pl.ds(other_at, CH)
            for lg in range(L):
                mr, mi = j32[lg * 2, at_m, :], j32[lg * 2 + 1, at_m, :]
                orr, oi = j32[lg * 2, at_o, :], j32[lg * 2 + 1, at_o, :]
                real = (mr * orr + mi * oi).astype(jnp.bfloat16)
                imag = (mi * orr - mr * oi).astype(jnp.bfloat16)
                top = slice(r * CH, (r + 1) * CH)
                low = slice((4 + r) * CH, (5 + r) * CH)
                one = slice(lg * 128, (lg + 1) * 128)
                two = slice(KQ + lg * 128, KQ + (lg + 1) * 128)
                x[top, one] = real
                x[top, two] = -imag
                x[low, one] = imag
                x[low, two] = real

        def multiply(n, _):
            at = pl.ds(pl.multiple_of(n * 256, 256), 256)
            value = jnp.dot(x[:, :KQ], table[2 * q, :, at], preferred_element_type=jnp.float32)
            value += jnp.dot(x[:, KQ:], table[2 * q + 1, :, at], preferred_element_type=jnp.float32)
            if q == 0:
                acc[:, at] = value
            else:
                acc[:, at] += value
            return 0

        lax.fori_loop(0, LAGS // 256, multiply, 0)

    weight = jnp.where(ylo == 0, keep[0], keep[1]).astype(jnp.float32)
    for b in range(2):
        for k in range(2):
            def stack(i, _):
                r = (b * 2 + k) * CH + i * 16
                real = acc[pl.ds(pl.multiple_of(r, 16), 16), :]
                imag = acc[pl.ds(pl.multiple_of(4 * CH + r, 16), 16), :]
                scale = weight * jnp.minimum(lax.rsqrt(real * real + imag * imag), 1.0 / FLOOR)
                at = pl.ds(pl.multiple_of(i * 16, 16), 16)
                s[0, b, k, at, :] = (weight * real).astype(jnp.bfloat16)
                s[1, b, k, at, :] = (scale * real).astype(jnp.bfloat16)
                s[2, b, k, at, :] = (scale * imag).astype(jnp.bfloat16)
                return 0

            lax.fori_loop(0, CH // 16, stack, 0)

    def rows16(i):
        return pl.ds(pl.multiple_of(i * 16, 16), 16)

    def rows32(i):
        return pl.ds(pl.multiple_of(i * 32, 32), 32)

    def cols512(i):
        return pl.ds(pl.multiple_of(i * 512, 512), 512)

    def cols256(i):
        return pl.ds(pl.multiple_of(i * 256, 256), 256)

    first_a = [
        send(s.at[:, :, 0, rows16(x_peer[d]), :], ra.at[d], x_dev[d]) for d in range(3)
    ]
    first_b = [
        send(s.at[:, lax.rem(y_peer[d], 2), 1, rows32(y_peer[d] // 2), :], rb.at[d], y_dev[d])
        for d in range(3)
    ]
    for copy in first_a:
        copy.wait_recv()
    for v in range(3):
        for b in range(2):
            total = s[v, b, 0, rows16(xx), :].astype(jnp.float32)
            for d in range(3):
                total += ra[d, v, b].astype(jnp.float32)
            pa[v, b] = total.astype(jnp.bfloat16)
    second_a = [
        send(pa.at[:, lax.rem(y_peer[d], 2), :, cols512(y_peer[d] // 2)], ra2.at[d], y_dev[d])
        for d in range(3)
    ]
    for copy in first_b:
        copy.wait_recv()
    for v in range(3):
        total = s[v, ylo, 1, rows32(yhi), :].astype(jnp.float32)
        for d in range(3):
            total += rb[d, v].astype(jnp.float32)
        pb[v] = total.astype(jnp.bfloat16)
    second_b = [
        send(pb.at[:, :, cols256(x_peer[d])], rb2.at[d], x_dev[d]) for d in range(3)
    ]

    def finish(parts):
        linear = parts[0] * (1.0 / 4.0)
        phased = linear * jnp.sqrt(parts[1] * parts[1] + parts[2] * parts[2]) * (1.0 / 16.0)
        return linear.astype(jnp.bfloat16), phased.astype(jnp.bfloat16)

    for copy in second_a:
        copy.wait_recv()
    parts = []
    for v in range(3):
        total = pa[v, ylo, :, cols512(yhi)].astype(jnp.float32)
        for d in range(3):
            total += ra2[d, v].astype(jnp.float32)
        parts.append(total)
    linear, phased = finish(parts)
    g[0, 0, rows16(xx), cols512(yhi)] = linear
    g[1, 0, rows16(xx), cols512(yhi)] = phased
    last = []
    piece = g.at[:, 0, rows16(xx), cols512(yhi)]
    for dev in g_dev:
        last.append(send(piece, piece, dev))
    for copy in second_b:
        copy.wait_recv()
    parts = []
    for v in range(3):
        total = pb[v, :, cols256(xx)].astype(jnp.float32)
        for d in range(3):
            total += rb2[d, v].astype(jnp.float32)
        parts.append(total)
    linear, phased = finish(parts)
    g[0, 1, rows32(yhi), cols256(xx)] = linear
    g[1, 1, rows32(yhi), cols256(xx)] = phased
    piece = g.at[:, 1, rows32(yhi), cols256(xx)]
    for dev in g_dev:
        last.append(send(piece, piece, dev))
    for copy in last:
        copy.wait_recv()

    for k in range(2):
        lin_out[k] = g[0, k].astype(jnp.float32)
        ph_out[k] = g[1, k].astype(jnp.float32)
    bins = jnp.dot(member[0], g[0, 0], preferred_element_type=jnp.float32)
    bins += jnp.dot(member[1], g[0, 1], preferred_element_type=jnp.float32)
    bin_out[...] = bins
    for copy in sent:
        copy.wait_send()


def stacks(wt, offs, keep, member):
    vmem = pl.BlockSpec(memory_space=pltpu.VMEM)
    smem = pl.BlockSpec(memory_space=pltpu.SMEM)
    bf16, f32 = jnp.bfloat16, jnp.float32
    copies = 5 * Q + 3 * Q + 3 * Q + 12 + 14
    block = (12, L, 2, CH, 128)
    return pl.pallas_call(
        kernel,
        out_shape=(
            jax.ShapeDtypeStruct((2, CH, LAGS), f32),
            jax.ShapeDtypeStruct((2, CH, LAGS), f32),
            jax.ShapeDtypeStruct((NBIN, LAGS), f32),
        ),
        in_specs=[pl.BlockSpec(memory_space=pl.ANY), smem, smem, vmem],
        out_specs=(vmem, vmem, vmem),
        scratch_shapes=[
            *[pltpu.VMEM(block, bf16)] * Q,
            pltpu.VMEM((2 * L, 12 * CH, 128), f32),
            pltpu.VMEM((2, F // FINE, LAGS), f32),
            pltpu.VMEM((2, FINE, LAGS), f32),
            pltpu.VMEM((2 * Q, KQ, LAGS), bf16),
            pltpu.VMEM((8 * CH, 2 * KQ), bf16),
            pltpu.VMEM((8 * CH, LAGS), f32),
            pltpu.VMEM((3, 2, 2, CH, LAGS), bf16),
            pltpu.VMEM((3, 3, 2, 16, LAGS), bf16),
            pltpu.VMEM((3, 3, 32, LAGS), bf16),
            pltpu.VMEM((3, 2, 16, LAGS), bf16),
            pltpu.VMEM((3, 32, LAGS), bf16),
            pltpu.VMEM((3, 3, 16, 512), bf16),
            pltpu.VMEM((3, 3, 32, 256), bf16),
            pltpu.VMEM((2, 2, CH, LAGS), bf16),
            pltpu.SemaphoreType.DMA((Q,)),
            pltpu.SemaphoreType.DMA((copies,)),
            pltpu.SemaphoreType.DMA((copies,)),
        ],
        compiler_params=pltpu.CompilerParams(
            collective_id=0, has_side_effects=True, vmem_limit_bytes=48 * 1024 * 1024
        ),
    )(wt, offs, keep, member)


def local(spectra, band_offsets, window_keep, chan_dist):
    win_dev, ch_dev, _, freqs = spectra.shape
    channels = ch_dev * lax.axis_size("chan")
    white = whiten(spectra)
    wt = white.reshape(win_dev, ch_dev, 2, freqs // 128, 128).transpose(0, 3, 2, 1, 4)
    pairs = [(i, i ^ 2) for i in range(lax.axis_size("chan"))]
    offs = jnp.concatenate([band_offsets, lax.ppermute(band_offsets, "chan", pairs)], axis=0)
    own = lax.axis_index("chan") * ch_dev + jnp.arange(ch_dev, dtype=jnp.int32)
    partner = jnp.mod(own[None, :] + band_offsets[0][:, None], channels)
    every = jnp.arange(channels, dtype=jnp.int32)
    own_dist = jnp.sum(jnp.where(own[:, None] == every[None, :], chan_dist[None, :], 0), axis=1)
    partner_dist = jnp.sum(
        jnp.where(partner[:, :, None] == every[None, None, :], chan_dist[None, None, :], 0), axis=2
    )
    bins = jnp.minimum(jnp.abs(partner_dist - own_dist[None, :]), NBIN - 1)
    member = (jnp.arange(NBIN, dtype=jnp.int32)[None, :, None] == bins[:, None, :]).astype(jnp.bfloat16)
    linear, phased, binned = stacks(wt, offs, window_keep, member)
    return (linear.transpose(1, 0, 2), phased.transpose(1, 0, 2), binned)


def solution(mesh):
    in_specs = (P("win", "chan", None, None), P("chan", None), P("win"), P())
    out_specs = (P("chan", None, None), P("chan", None, None), P("chan", None))
    return jax.shard_map(local, mesh=mesh, in_specs=in_specs, out_specs=out_specs, check_vma=False)
```

```python
import functools
import math

import jax
import jax.numpy as jnp
from jax import lax
from jax.experimental import pallas as pl
from jax.experimental.pallas import tpu as pltpu
from jax.sharding import PartitionSpec as P

LAGS = 1024
NBIN = 32
EPS = 1e-06
FLOOR = 0.1

F = 2048
CH = 64
Q = 4
L = F // 128 // Q
KQ = L * 128
FINE = 32
LIFT = 2.0**20
MESH = pl.DeviceIdType.MESH


def turn(product):
    return jnp.bitwise_and(product, 2 * F - 1).astype(jnp.float32) * (math.pi / F)


def kernel(
    wt, offs, keep, dist,
    lin_out, ph_out, bin_out,
    j0, j1, j2, j3, far_offs, j32, power_m, power_o, member, ea, eb, table, x, acc, s,
    ra, rb, pa, pb, ra2, rb2, g,
    local_sem, send_sem, recv_sem,
):
    joined = (j0, j1, j2, j3)
    chan = lax.axis_index("chan")
    win = lax.axis_index("win")
    core = lax.rem(chan, 2)
    ylo = lax.rem(chan // 2, 2)
    xx = win // 2
    yhi = lax.rem(win, 2)
    yy = yhi * 2 + ylo
    base = chan - ylo * 2
    above = lax.rem(chan + 4, 32)
    below = lax.rem(chan + 28, 32)
    mate = chan + 1 - 2 * core
    across = chan + 2 - 4 * ylo
    own = ylo * 2 + core
    far = (1 - ylo) * 2 + core

    x_peer = [lax.rem(xx + d, 4) for d in (1, 2, 3)]
    y_peer = [lax.rem(yy + d, 4) for d in (1, 2, 3)]
    x_dev = [{"chan": chan, "win": p * 2 + yhi} for p in x_peer]
    y_dev = [{"chan": base + lax.rem(p, 2) * 2, "win": xx * 2 + p // 2} for p in y_peer]
    g_dev = [{"chan": chan, "win": win + 1 - 2 * yhi}] + [
        dev for p in x_peer for dev in (
            {"chan": chan, "win": p * 2 + yhi}, {"chan": chan, "win": p * 2 + 1 - yhi})
    ]

    barrier = pltpu.get_barrier_semaphore()
    greet = [{"chan": c, "win": win} for c in (above, below, mate)] + y_dev + x_dev + [
        {"chan": chan, "win": p * 2 + 1 - yhi} for p in x_peer
    ]
    for dev in greet:
        pl.semaphore_signal(barrier, inc=1, device_id=dev, device_id_type=MESH)
    pl.semaphore_wait(barrier, len(greet))

    count = [0]
    sent = []

    def send(src, dst, device):
        i = count[0]
        count[0] += 1
        copy = pltpu.make_async_remote_copy(
            src_ref=src, dst_ref=dst, send_sem=send_sem.at[i], recv_sem=recv_sem.at[i],
            device_id=device, device_id_type=MESH,
        )
        copy.start()
        sent.append(copy)
        return copy

    def near(c):
        return {"chan": c, "win": win}

    offs_copy = send(offs, far_offs, near(across))
    lanes = [pl.ds(q * L, L) for q in range(Q)]
    stay, cross_y, up, down, mate_own = [], [], [], [], []
    for q in range(Q):
        mine = wt.at[ylo, lanes[q]]
        copy = pltpu.make_async_copy(mine, joined[q].at[4 + own], local_sem.at[q])
        copy.start()
        stay.append(copy)
        cross_y.append(send(wt.at[1 - ylo, lanes[q]], joined[q].at[4 + own], near(across)))
        up.append(send(mine, joined[q].at[own], near(above)))
        down.append(send(mine, joined[q].at[8 + own], near(below)))
        mate_own.append(send(mine, joined[q].at[4 + own], near(mate)))

    lag = lax.broadcasted_iota(jnp.int32, (FINE, LAGS), 1) - LAGS // 2
    row = lax.broadcasted_iota(jnp.int32, (FINE, LAGS), 0)
    fine = turn(row * lag)
    eb[0] = jnp.cos(fine) * (1.0 / math.sqrt(F))
    eb[1] = jnp.sin(fine) * (1.0 / math.sqrt(F))
    for half in range(F // FINE // FINE):
        coarse = turn((row + half * FINE) * FINE * lag)
        ea[0, half * FINE:(half + 1) * FINE] = jnp.cos(coarse)
        ea[1, half * FINE:(half + 1) * FINE] = jnp.sin(coarse)

    per = KQ // FINE

    def fill(a, _):
        ca = ea[0, pl.ds(a, 1), :]
        sa = ea[1, pl.ds(a, 1), :]
        q2 = (a // per) * 2
        at = pl.ds(pl.multiple_of(lax.rem(a, per) * FINE, FINE), FINE)
        table[q2, at, :] = (eb[0] * ca - eb[1] * sa).astype(jnp.bfloat16)
        table[q2 + 1, at, :] = (eb[1] * ca + eb[0] * sa).astype(jnp.bfloat16)
        return 0

    lax.fori_loop(0, F // FINE, fill, 0)

    place = chan * CH + lax.broadcasted_iota(jnp.int32, (CH, 1), 0)
    every = lax.broadcasted_iota(jnp.int32, (CH, 32 * CH), 1)
    row_dist = dist[...].astype(jnp.float32)

    def distance(index):
        return jnp.sum(jnp.where(every == index, row_dist, 0.0), axis=1, keepdims=True)

    own_dist = distance(place)
    for k in range(2):
        partner = jnp.bitwise_and(place + offs[0, k], 32 * CH - 1)
        bins = jnp.minimum(jnp.abs(distance(partner) - own_dist), NBIN - 1.0)
        column = lax.broadcasted_iota(jnp.int32, (CH, 128), 1).astype(jnp.float32)
        member[k] = (bins == column).astype(jnp.float32)

    offs_copy.wait_recv()
    up_far, down_far, mate_far = [], [], []
    for q in range(Q):
        cross_y[q].wait_recv()
        mine = joined[q].at[4 + far]
        up_far.append(send(mine, joined[q].at[far], near(above)))
        down_far.append(send(mine, joined[q].at[8 + far], near(below)))
        mate_far.append(send(mine, joined[q].at[4 + far], near(mate)))

    def forward(q):
        for copy in (up[q], down[q], up_far[q], down_far[q]):
            copy.wait_recv()
        return [
            send(joined[q].at[pos], joined[q].at[pos], near(mate))
            for pos in (2 + core, 8 + core, 10 - 9 * core)
        ]

    starts = []
    for b in range(2):
        block = core + 2 * b
        for k in range(2):
            starts.append(((4 + block) * CH, (4 + block) * CH + jnp.where(
                block == own, offs[0, k], far_offs[0, k])))

    for q in range(Q):
        moved = forward(q)
        stay[q].wait()
        mate_own[q].wait_recv()
        mate_far[q].wait_recv()
        for copy in moved:
            copy.wait_recv()

        def widen(i, _):
            p = core + i
            at = pl.ds(pl.multiple_of(p * CH, CH), CH)
            for lg in range(L):
                for ri in range(2):
                    j32[lg * 2 + ri, at, :] = joined[q][p, lg, ri].astype(jnp.float32)
            return 0

        lax.fori_loop(0, 11, widen, 0)
        for r, (mine_at, other_at) in enumerate(starts):
            at_m = pl.ds(pl.multiple_of(mine_at, CH), CH)
            at_o = pl.ds(other_at, CH)
            sum_m, sum_o = None, None
            for lg in range(L):
                mr, mi = j32[lg * 2, at_m, :], j32[lg * 2 + 1, at_m, :]
                orr, oi = j32[lg * 2, at_o, :], j32[lg * 2 + 1, at_o, :]
                square = orr * orr + oi * oi
                sum_o = square if sum_o is None else sum_o + square
                if r % 2 == 0:
                    square = mr * mr + mi * mi
                    sum_m = square if sum_m is None else sum_m + square
                mr, mi = mr * LIFT, mi * LIFT
                real = (mr * orr + mi * oi).astype(jnp.bfloat16)
                imag = (mi * orr - mr * oi).astype(jnp.bfloat16)
                top = slice(r * CH, (r + 1) * CH)
                low = slice((4 + r) * CH, (5 + r) * CH)
                one = slice(lg * 128, (lg + 1) * 128)
                two = slice(KQ + lg * 128, KQ + (lg + 1) * 128)
                x[top, one] = real
                x[top, two] = -imag
                x[low, one] = imag
                x[low, two] = real
            power_o[r] = sum_o if q == 0 else power_o[r] + sum_o
            if r % 2 == 0:
                power_m[r // 2] = sum_m if q == 0 else power_m[r // 2] + sum_m

        def multiply(n, _):
            at = pl.ds(pl.multiple_of(n * 256, 256), 256)
            value = jnp.dot(x[:, :KQ], table[2 * q, :, at], preferred_element_type=jnp.float32)
            value += jnp.dot(x[:, KQ:], table[2 * q + 1, :, at], preferred_element_type=jnp.float32)
            if q == 0:
                acc[:, at] = value
            else:
                acc[:, at] += value
            return 0

        lax.fori_loop(0, LAGS // 256, multiply, 0)

    weight = jnp.where(ylo == 0, keep[0], keep[1]).astype(jnp.float32)
    for b in range(2):
        for k in range(2):
            def stack(i, _):
                r = (b * 2 + k) * CH + i * 16
                at = pl.ds(pl.multiple_of(i * 16, 16), 16)
                mean_m = jnp.sum(power_m[b, at, :], axis=1, keepdims=True) * (1.0 / F)
                mean_o = jnp.sum(power_o[b * 2 + k, at, :], axis=1, keepdims=True) * (1.0 / F)
                gain = lax.rsqrt(mean_m + EPS) * (1.0 / LIFT) * lax.rsqrt(mean_o + EPS)
                real = acc[pl.ds(pl.multiple_of(r, 16), 16), :] * gain
                imag = acc[pl.ds(pl.multiple_of(4 * CH + r, 16), 16), :] * gain
                scale = weight * jnp.minimum(lax.rsqrt(real * real + imag * imag), 1.0 / FLOOR)
                s[0, b, k, at, :] = (weight * real).astype(jnp.bfloat16)
                s[1, b, k, at, :] = (scale * real).astype(jnp.bfloat16)
                s[2, b, k, at, :] = (scale * imag).astype(jnp.bfloat16)
                return 0

            lax.fori_loop(0, CH // 16, stack, 0)

    def rows16(i):
        return pl.ds(pl.multiple_of(i * 16, 16), 16)

    def rows32(i):
        return pl.ds(pl.multiple_of(i * 32, 32), 32)

    def cols512(i):
        return pl.ds(pl.multiple_of(i * 512, 512), 512)

    def cols256(i):
        return pl.ds(pl.multiple_of(i * 256, 256), 256)

    first_a = [
        send(s.at[:, :, 0, rows16(x_peer[d]), :], ra.at[d], x_dev[d]) for d in range(3)
    ]
    first_b = [
        send(s.at[:, lax.rem(y_peer[d], 2), 1, rows32(y_peer[d] // 2), :], rb.at[d], y_dev[d])
        for d in range(3)
    ]
    for copy in first_a:
        copy.wait_recv()
    for v in range(3):
        for b in range(2):
            total = s[v, b, 0, rows16(xx), :].astype(jnp.float32)
            for d in range(3):
                total += ra[d, v, b].astype(jnp.float32)
            pa[v, b] = total.astype(jnp.bfloat16)
    second_a = [
        send(pa.at[:, lax.rem(y_peer[d], 2), :, cols512(y_peer[d] // 2)], ra2.at[d], y_dev[d])
        for d in range(3)
    ]
    for copy in first_b:
        copy.wait_recv()
    for v in range(3):
        total = s[v, ylo, 1, rows32(yhi), :].astype(jnp.float32)
        for d in range(3):
            total += rb[d, v].astype(jnp.float32)
        pb[v] = total.astype(jnp.bfloat16)
    second_b = [
        send(pb.at[:, :, cols256(x_peer[d])], rb2.at[d], x_dev[d]) for d in range(3)
    ]

    def finish(parts):
        linear = parts[0] * (1.0 / 4.0)
        phased = linear * jnp.sqrt(parts[1] * parts[1] + parts[2] * parts[2]) * (1.0 / 16.0)
        return linear.astype(jnp.bfloat16), phased.astype(jnp.bfloat16)

    for copy in second_a:
        copy.wait_recv()
    parts = []
    for v in range(3):
        total = pa[v, ylo, :, cols512(yhi)].astype(jnp.float32)
        for d in range(3):
            total += ra2[d, v].astype(jnp.float32)
        parts.append(total)
    linear, phased = finish(parts)
    g[0, 0, rows16(xx), cols512(yhi)] = linear
    g[1, 0, rows16(xx), cols512(yhi)] = phased
    last = []
    piece = g.at[:, 0, rows16(xx), cols512(yhi)]
    for dev in g_dev:
        last.append(send(piece, piece, dev))
    for copy in second_b:
        copy.wait_recv()
    parts = []
    for v in range(3):
        total = pb[v, :, cols256(xx)].astype(jnp.float32)
        for d in range(3):
            total += rb2[d, v].astype(jnp.float32)
        parts.append(total)
    linear, phased = finish(parts)
    g[0, 1, rows32(yhi), cols256(xx)] = linear
    g[1, 1, rows32(yhi), cols256(xx)] = phased
    piece = g.at[:, 1, rows32(yhi), cols256(xx)]
    for dev in g_dev:
        last.append(send(piece, piece, dev))
    for copy in last:
        copy.wait_recv()

    for k in range(2):
        lin_out[k] = g[0, k].astype(jnp.float32)
        ph_out[k] = g[1, k].astype(jnp.float32)
    bins = jnp.zeros((128, LAGS), jnp.float32)
    for k in range(2):
        bins += lax.dot_general(
            member[k].astype(jnp.bfloat16), g[0, k], (((0,), (0,)), ((), ())),
            preferred_element_type=jnp.float32,
        )
    bin_out[...] = bins[:NBIN]
    for copy in sent:
        copy.wait_send()


def stacks(wt, offs, keep, dist):
    vmem = pl.BlockSpec(memory_space=pltpu.VMEM)
    smem = pl.BlockSpec(memory_space=pltpu.SMEM)
    bf16, f32 = jnp.bfloat16, jnp.float32
    copies = 1 + 5 * Q + 3 * Q + 3 * Q + 12 + 14
    block = (12, L, 2, CH, 128)
    return pl.pallas_call(
        kernel,
        out_shape=(
            jax.ShapeDtypeStruct((2, CH, LAGS), f32),
            jax.ShapeDtypeStruct((2, CH, LAGS), f32),
            jax.ShapeDtypeStruct((NBIN, LAGS), f32),
        ),
        in_specs=[pl.BlockSpec(memory_space=pl.ANY), smem, smem, vmem],
        out_specs=(vmem, vmem, vmem),
        scratch_shapes=[
            *[pltpu.VMEM(block, bf16)] * Q,
            pltpu.SMEM((1, 2), jnp.int32),
            pltpu.VMEM((2 * L, 12 * CH, 128), f32),
            pltpu.VMEM((2, CH, 128), f32),
            pltpu.VMEM((4, CH, 128), f32),
            pltpu.VMEM((2, CH, 128), f32),
            pltpu.VMEM((2, F // FINE, LAGS), f32),
            pltpu.VMEM((2, FINE, LAGS), f32),
            pltpu.VMEM((2 * Q, KQ, LAGS), bf16),
            pltpu.VMEM((8 * CH, 2 * KQ), bf16),
            pltpu.VMEM((8 * CH, LAGS), f32),
            pltpu.VMEM((3, 2, 2, CH, LAGS), bf16),
            pltpu.VMEM((3, 3, 2, 16, LAGS), bf16),
            pltpu.VMEM((3, 3, 32, LAGS), bf16),
            pltpu.VMEM((3, 2, 16, LAGS), bf16),
            pltpu.VMEM((3, 32, LAGS), bf16),
            pltpu.VMEM((3, 3, 16, 512), bf16),
            pltpu.VMEM((3, 3, 32, 256), bf16),
            pltpu.VMEM((2, 2, CH, LAGS), bf16),
            pltpu.SemaphoreType.DMA((Q,)),
            pltpu.SemaphoreType.DMA((copies,)),
            pltpu.SemaphoreType.DMA((copies,)),
        ],
        compiler_params=pltpu.CompilerParams(
            collective_id=0, has_side_effects=True, vmem_limit_bytes=48 * 1024 * 1024
        ),
    )(wt, offs, keep, dist)


def local(spectra, band_offsets, window_keep, chan_dist):
    win_dev, ch_dev, _, freqs = spectra.shape
    wt = spectra.reshape(win_dev, ch_dev, 2, freqs // 128, 128).transpose(0, 3, 2, 1, 4)
    linear, phased, binned = stacks(wt, band_offsets, window_keep, chan_dist[None, :])
    return (linear.transpose(1, 0, 2), phased.transpose(1, 0, 2), binned)


def solution(mesh):
    in_specs = (P("win", "chan", None, None), P("chan", None), P("win"), P())
    out_specs = (P("chan", None, None), P("chan", None, None), P("chan", None))
    return jax.shard_map(local, mesh=mesh, in_specs=in_specs, out_specs=out_specs, check_vma=False)
```

```python
import functools
import math

import jax
import jax.numpy as jnp
from jax import lax
from jax.experimental import pallas as pl
from jax.experimental.pallas import tpu as pltpu
from jax.sharding import PartitionSpec as P

LAGS = 1024
NBIN = 32
EPS = 1e-06
FLOOR = 0.1

F = 2048
CH = 64
Q = 4
L = F // 128 // Q
KQ = L * 128
FINE = 32
LIFT = 2.0**20
MESH = pl.DeviceIdType.MESH


def turn(product):
    return jnp.bitwise_and(product, 2 * F - 1).astype(jnp.float32) * (math.pi / F)


def kernel(
    wt, offs, keep, dist,
    lin_out, ph_out, bin_out,
    j0, j1, j2, j3, far_offs, j32, power_m, power_o, member, ea, eb, table, x, acc,
    s_early, s_late, ra_early, ra_late, pa_early, pa_late, rb, pb, ra2, rb2, g,
    local_sem, send_sem, recv_sem,
):
    joined = (j0, j1, j2, j3)
    chan = lax.axis_index("chan")
    win = lax.axis_index("win")
    core = lax.rem(chan, 2)
    ylo = lax.rem(chan // 2, 2)
    xx = win // 2
    yhi = lax.rem(win, 2)
    above = lax.rem(chan + 4, 32)
    below = lax.rem(chan + 28, 32)
    mate = chan + 1 - 2 * core
    across = chan + 2 - 4 * ylo
    own = ylo * 2 + core
    far = (1 - ylo) * 2 + core
    first_way = jnp.where(ylo == 1, above, below)
    other_way = jnp.where(ylo == 1, below, above)
    early_way = jnp.where(core == 0, below, above)
    late_way = jnp.where(core == 0, above, below)
    early = 2 - core
    late = 3 * core
    owns_early = ylo + core == 1
    owns_late = ylo == core

    x_peer = [lax.rem(xx + d, 4) for d in (1, 2, 3)]
    x_dev = [{"chan": chan, "win": p * 2 + yhi} for p in x_peer]
    y_dev = [
        {"chan": chan, "win": win + 1 - 2 * yhi},
        {"chan": across, "win": win},
        {"chan": across, "win": win + 1 - 2 * yhi},
    ]
    y_half = [1 - yhi, yhi, 1 - yhi]
    far_x = [{"chan": chan, "win": p * 2 + 1 - yhi} for p in x_peer]
    g_dev = [y_dev[0]] + x_dev + far_x

    barrier = pltpu.get_barrier_semaphore()
    greet = [{"chan": c, "win": win} for c in (above, below, mate)] + y_dev + x_dev + far_x
    for dev in greet:
        pl.semaphore_signal(barrier, inc=1, device_id=dev, device_id_type=MESH)
    pl.semaphore_wait(barrier, len(greet))

    count = [0]
    sent = []

    def make(src, dst, device, when=None):
        i = count[0]
        count[0] += 1
        copy = pltpu.make_async_remote_copy(
            src_ref=src, dst_ref=dst, send_sem=send_sem.at[i], recv_sem=recv_sem.at[i],
            device_id=device, device_id_type=MESH,
        )
        sent.append((when, copy))
        return copy

    def send(*args, **kwargs):
        copy = make(*args, **kwargs)
        copy.start()
        return copy

    def near(c):
        return {"chan": c, "win": win}

    offs_copy = send(offs, far_offs, near(across))
    lanes = [pl.ds(q * L, L) for q in range(Q)]
    stay, cross_y, own_first, mate_own = [], [], [], []
    for q in range(Q):
        mine = wt.at[ylo, lanes[q]]
        copy = pltpu.make_async_copy(mine, joined[q].at[4 + own], local_sem.at[q])
        copy.start()
        stay.append(copy)
        cross_y.append(send(wt.at[1 - ylo, lanes[q]], joined[q].at[4 + own], near(across)))
        own_first.append(send(mine, joined[q].at[8 + core - 6 * ylo], near(first_way)))
        mate_own.append(send(mine, joined[q].at[4 + own], near(mate)))
    for_early = [
        make(joined[q].at[4 + early], joined[q].at[10 - 9 * core], near(early_way)) for q in range(Q)
    ]
    for_late = [
        make(joined[q].at[4 + late], joined[q].at[11 * core], near(late_way)) for q in range(Q)
    ]
    for copy in stay:
        copy.wait()

    @pl.when(owns_early)
    def _():
        for_early[0].start()

    @pl.when(owns_late)
    def _():
        for_late[0].start()

    lag = lax.broadcasted_iota(jnp.int32, (FINE, LAGS), 1) - LAGS // 2
    row = lax.broadcasted_iota(jnp.int32, (FINE, LAGS), 0)
    fine = turn(row * lag)
    eb[0] = jnp.cos(fine) * (1.0 / math.sqrt(F))
    eb[1] = jnp.sin(fine) * (1.0 / math.sqrt(F))
    for half in range(F // FINE // FINE):
        coarse = turn((row + half * FINE) * FINE * lag)
        ea[0, half * FINE:(half + 1) * FINE] = jnp.cos(coarse)
        ea[1, half * FINE:(half + 1) * FINE] = jnp.sin(coarse)

    per = KQ // FINE

    def fill(a, _):
        ca = ea[0, pl.ds(a, 1), :]
        sa = ea[1, pl.ds(a, 1), :]
        q2 = (a // per) * 2
        at = pl.ds(pl.multiple_of(lax.rem(a, per) * FINE, FINE), FINE)
        table[q2, at, :] = (eb[0] * ca - eb[1] * sa).astype(jnp.bfloat16)
        table[q2 + 1, at, :] = (eb[1] * ca + eb[0] * sa).astype(jnp.bfloat16)
        return 0

    far_first, mate_far = [], []
    for q in range(Q):
        cross_y[q].wait_recv()
        mine = joined[q].at[4 + far]
        far_first.append(send(mine, joined[q].at[2 + core + 6 * ylo], near(other_way)))
        mate_far.append(send(mine, joined[q].at[4 + far], near(mate)))
        lax.fori_loop(q * per, (q + 1) * per, fill, 0)

    @pl.when(owns_late)
    def _():
        for_early[0].start()

    for q in range(1, Q):
        for_early[q].start()

    place = chan * CH + lax.broadcasted_iota(jnp.int32, (CH, 1), 0)
    every = lax.broadcasted_iota(jnp.int32, (CH, 32 * CH), 1)
    row_dist = dist[...].astype(jnp.float32)

    def distance(index):
        return jnp.sum(jnp.where(every == index, row_dist, 0.0), axis=1, keepdims=True)

    own_dist = distance(place)
    for k in range(2):
        partner = jnp.bitwise_and(place + offs[0, k], 32 * CH - 1)
        bins = jnp.minimum(jnp.abs(distance(partner) - own_dist), NBIN - 1.0)
        column = lax.broadcasted_iota(jnp.int32, (CH, 128), 1).astype(jnp.float32)
        member[k] = (bins == column).astype(jnp.float32)

    offs_copy.wait_recv()
    forward = []
    for q in range(Q):
        own_first[q].wait_recv()
        far_first[q].wait_recv()
        forward.append([
            send(joined[q].at[pos], joined[q].at[pos], near(mate)) for pos in (2 + core, 8 + core)
        ])

    def widen(q, first, number):
        def one(i, _):
            p = first + i
            at = pl.ds(pl.multiple_of(p * CH, CH), CH)
            for lg in range(L):
                for ri in range(2):
                    j32[(q * L + lg) * 2 + ri, at, :] = joined[q][p, lg, ri].astype(jnp.float32)
            return 0

        lax.fori_loop(0, number, one, 0)

    def correlate(q, h, block, owns):
        at_m = pl.ds(pl.multiple_of((4 + block) * CH, CH), CH)
        for k in range(2):
            at_o = pl.ds((4 + block) * CH + jnp.where(owns, offs[0, k], far_offs[0, k]), CH)
            sum_m, sum_o = None, None
            for lg in range(L):
                j = (q * L + lg) * 2
                mr, mi = j32[j, at_m, :], j32[j + 1, at_m, :]
                orr, oi = j32[j, at_o, :], j32[j + 1, at_o, :]
                square = orr * orr + oi * oi
                sum_o = square if sum_o is None else sum_o + square
                if k == 0:
                    square = mr * mr + mi * mi
                    sum_m = square if sum_m is None else sum_m + square
                mr, mi = mr * LIFT, mi * LIFT
                real = (mr * orr + mi * oi).astype(jnp.bfloat16)
                imag = (mi * orr - mr * oi).astype(jnp.bfloat16)
                top = slice(k * CH, (k + 1) * CH)
                low = slice((2 + k) * CH, (3 + k) * CH)
                one = slice(lg * 128, (lg + 1) * 128)
                two = slice(KQ + lg * 128, KQ + (lg + 1) * 128)
                x[top, one] = real
                x[top, two] = -imag
                x[low, one] = imag
                x[low, two] = real
            power_o[h * 2 + k] = sum_o if q == 0 else power_o[h * 2 + k] + sum_o
            if k == 0:
                power_m[h] = sum_m if q == 0 else power_m[h] + sum_m

        def multiply(n, _):
            at = pl.ds(pl.multiple_of(n * 256, 256), 256)
            value = jnp.dot(x[:, :KQ], table[2 * q, :, at], preferred_element_type=jnp.float32)
            value += jnp.dot(x[:, KQ:], table[2 * q + 1, :, at], preferred_element_type=jnp.float32)
            if q == 0:
                acc[:, at] = value
            else:
                acc[:, at] += value
            return 0

        lax.fori_loop(0, LAGS // 256, multiply, 0)

    weight = jnp.where(ylo == 0, keep[0], keep[1]).astype(jnp.float32)

    def stack(h, s):
        for k in range(2):
            def one(i, _):
                r = k * CH + i * 16
                at = pl.ds(pl.multiple_of(i * 16, 16), 16)
                mean_m = jnp.sum(power_m[h, at, :], axis=1, keepdims=True) * (1.0 / F)
                mean_o = jnp.sum(power_o[h * 2 + k, at, :], axis=1, keepdims=True) * (1.0 / F)
                gain = lax.rsqrt(mean_m + EPS) * (1.0 / LIFT) * lax.rsqrt(mean_o + EPS)
                real = acc[pl.ds(pl.multiple_of(r, 16), 16), :] * gain
                imag = acc[pl.ds(pl.multiple_of(2 * CH + r, 16), 16), :] * gain
                scale = weight * jnp.minimum(lax.rsqrt(real * real + imag * imag), 1.0 / FLOOR)
                s[0, k, at, :] = (weight * real).astype(jnp.bfloat16)
                s[1, k, at, :] = (scale * real).astype(jnp.bfloat16)
                s[2, k, at, :] = (scale * imag).astype(jnp.bfloat16)
                return 0

            lax.fori_loop(0, CH // 16, one, 0)

    def rows16(i):
        return pl.ds(pl.multiple_of(i * 16, 16), 16)

    def rows32(i):
        return pl.ds(pl.multiple_of(i * 32, 32), 32)

    def cols512(i):
        return pl.ds(pl.multiple_of(i * 512, 512), 512)

    def cols256(i):
        return pl.ds(pl.multiple_of(i * 256, 256), 256)

    def to_owners(source, target, owns):
        copies = [
            make(source(y_half[n]), target.at[n], y_dev[n], when=owns if n == 0 else ~owns)
            for n in range(3)
        ]

        @pl.when(owns)
        def _():
            copies[0].start()

        @pl.when(~owns)
        def _():
            copies[1].start()
            copies[2].start()

        return copies

    def first_sums(s, ra, owns):
        a = [send(s.at[:, 0, rows16(x_peer[d]), :], ra.at[d], x_dev[d]) for d in range(3)]
        b = to_owners(lambda half: s.at[:, 1, rows32(half), :], rb, owns)
        return a, b

    def second_sums(s, ra, pa, owns, copies):
        a, b = copies
        for copy in a:
            copy.wait_recv()
        for v in range(3):
            total = s[v, 0, rows16(xx), :].astype(jnp.float32)
            for d in range(3):
                total += ra[d, v].astype(jnp.float32)
            pa[v] = total.astype(jnp.bfloat16)
        a2 = to_owners(lambda half: pa.at[:, :, cols512(half)], ra2, owns)
        b2 = [make(pb.at[:, :, cols256(x_peer[d])], rb2.at[d], x_dev[d], when=owns) for d in range(3)]

        @pl.when(owns)
        def _():
            for copy in b:
                copy.wait_recv()
            for v in range(3):
                total = s[v, 1, rows32(yhi), :].astype(jnp.float32)
                for d in range(3):
                    total += rb[d, v].astype(jnp.float32)
                pb[v] = total.astype(jnp.bfloat16)
            for copy in b2:
                copy.start()

        return a2, b2

    def finish(parts):
        linear = parts[0] * (1.0 / 4.0)
        phased = linear * jnp.sqrt(parts[1] * parts[1] + parts[2] * parts[2]) * (1.0 / 16.0)
        return linear.astype(jnp.bfloat16), phased.astype(jnp.bfloat16)

    piece_a = g.at[:, 0, rows16(xx), cols512(yhi)]
    piece_b = g.at[:, 1, rows32(yhi), cols256(xx)]
    last_a = [make(piece_a, piece_a, dev) for dev in g_dev]
    last_b = [make(piece_b, piece_b, dev) for dev in g_dev]

    def results(pa, owns, copies):
        a2, b2 = copies

        @pl.when(owns)
        def _():
            for copy in a2:
                copy.wait_recv()
            parts = []
            for v in range(3):
                total = pa[v, :, cols512(yhi)].astype(jnp.float32)
                for d in range(3):
                    total += ra2[d, v].astype(jnp.float32)
                parts.append(total)
            linear, phased = finish(parts)
            g[0, 0, rows16(xx), cols512(yhi)] = linear
            g[1, 0, rows16(xx), cols512(yhi)] = phased
            for copy in last_a:
                copy.start()
            for copy in b2:
                copy.wait_recv()
            parts = []
            for v in range(3):
                total = pb[v, :, cols256(xx)].astype(jnp.float32)
                for d in range(3):
                    total += rb2[d, v].astype(jnp.float32)
                parts.append(total)
            linear, phased = finish(parts)
            g[0, 1, rows32(yhi), cols256(xx)] = linear
            g[1, 1, rows32(yhi), cols256(xx)] = phased
            for copy in last_b:
                copy.start()

    pass_on = []
    for q in range(Q):
        mate_own[q].wait_recv()
        mate_far[q].wait_recv()
        for copy in forward[q]:
            copy.wait_recv()
        for_early[q].wait_recv()
        pos = 10 - 9 * core
        pass_on.append(send(joined[q].at[pos], joined[q].at[pos], near(mate)))
        if q == 0:
            @pl.when(owns_early)
            def _():
                for_late[0].start()
        else:
            for_late[q].start()
        widen(q, 2 - core, 9)
        correlate(q, 0, early, owns_early)
    stack(0, s_early)
    early_first = first_sums(s_early, ra_early, owns_early)
    for q in range(Q):
        pass_on[q].wait_recv()
        for_late[q].wait_recv()
        widen(q, 10 * core, 2)
        correlate(q, 1, late, owns_late)
        if q == 1:
            early_second = second_sums(s_early, ra_early, pa_early, owns_early, early_first)
    stack(1, s_late)
    late_first = first_sums(s_late, ra_late, owns_late)
    results(pa_early, owns_early, early_second)
    late_second = second_sums(s_late, ra_late, pa_late, owns_late, late_first)
    results(pa_late, owns_late, late_second)

    for copy in last_a + last_b:
        copy.wait_recv()
    for k in range(2):
        lin_out[k] = g[0, k].astype(jnp.float32)
        ph_out[k] = g[1, k].astype(jnp.float32)
    bins = jnp.zeros((128, LAGS), jnp.float32)
    for k in range(2):
        bins += lax.dot_general(
            member[k].astype(jnp.bfloat16), g[0, k], (((0,), (0,)), ((), ())),
            preferred_element_type=jnp.float32,
        )
    bin_out[...] = bins[:NBIN]
    for when, copy in sent:
        if when is None:
            copy.wait_send()
        else:
            pl.when(when)(copy.wait_send)


def stacks(wt, offs, keep, dist):
    vmem = pl.BlockSpec(memory_space=pltpu.VMEM)
    smem = pl.BlockSpec(memory_space=pltpu.SMEM)
    bf16, f32 = jnp.bfloat16, jnp.float32
    copies = 1 + 10 * Q + 2 * 12 + 14
    block = (12, L, 2, CH, 128)
    return pl.pallas_call(
        kernel,
        out_shape=(
            jax.ShapeDtypeStruct((2, CH, LAGS), f32),
            jax.ShapeDtypeStruct((2, CH, LAGS), f32),
            jax.ShapeDtypeStruct((NBIN, LAGS), f32),
        ),
        in_specs=[pl.BlockSpec(memory_space=pl.ANY), smem, smem, vmem],
        out_specs=(vmem, vmem, vmem),
        scratch_shapes=[
            *[pltpu.VMEM(block, bf16)] * Q,
            pltpu.SMEM((1, 2), jnp.int32),
            pltpu.VMEM((Q * 2 * L, 12 * CH, 128), f32),
            pltpu.VMEM((2, CH, 128), f32),
            pltpu.VMEM((4, CH, 128), f32),
            pltpu.VMEM((2, CH, 128), f32),
            pltpu.VMEM((2, F // FINE, LAGS), f32),
            pltpu.VMEM((2, FINE, LAGS), f32),
            pltpu.VMEM((2 * Q, KQ, LAGS), bf16),
            pltpu.VMEM((4 * CH, 2 * KQ), bf16),
            pltpu.VMEM((4 * CH, LAGS), f32),
            pltpu.VMEM((3, 2, CH, LAGS), bf16),
            pltpu.VMEM((3, 2, CH, LAGS), bf16),
            pltpu.VMEM((3, 3, 16, LAGS), bf16),
            pltpu.VMEM((3, 3, 16, LAGS), bf16),
            pltpu.VMEM((3, 16, LAGS), bf16),
            pltpu.VMEM((3, 16, LAGS), bf16),
            pltpu.VMEM((3, 3, 32, LAGS), bf16),
            pltpu.VMEM((3, 32, LAGS), bf16),
            pltpu.VMEM((3, 3, 16, 512), bf16),
            pltpu.VMEM((3, 3, 32, 256), bf16),
            pltpu.VMEM((2, 2, CH, LAGS), bf16),
            pltpu.SemaphoreType.DMA((Q,)),
            pltpu.SemaphoreType.DMA((copies,)),
            pltpu.SemaphoreType.DMA((copies,)),
        ],
        compiler_params=pltpu.CompilerParams(
            collective_id=0, has_side_effects=True, vmem_limit_bytes=52 * 1024 * 1024
        ),
    )(wt, offs, keep, dist)


def local(spectra, band_offsets, window_keep, chan_dist):
    win_dev, ch_dev, _, freqs = spectra.shape
    wt = spectra.reshape(win_dev, ch_dev, 2, freqs // 128, 128).transpose(0, 3, 2, 1, 4)
    linear, phased, binned = stacks(wt, band_offsets, window_keep, chan_dist[None, :])
    return (linear.transpose(1, 0, 2), phased.transpose(1, 0, 2), binned)


def solution(mesh):
    in_specs = (P("win", "chan", None, None), P("chan", None), P("win"), P())
    out_specs = (P("chan", None, None), P("chan", None, None), P("chan", None))
    return jax.shard_map(local, mesh=mesh, in_specs=in_specs, out_specs=out_specs, check_vma=False)
```

```python
import functools
import math

import jax
import jax.numpy as jnp
from jax import lax
from jax.experimental import pallas as pl
from jax.experimental.pallas import tpu as pltpu
from jax.sharding import PartitionSpec as P

LAGS = 1024
NBIN = 32
EPS = 1e-06
FLOOR = 0.1

F = 2048
CH = 64
Q = 4
L = F // 128 // Q
KQ = L * 128
FINE = 32
LIFT = 2.0**20
MESH = pl.DeviceIdType.MESH


def turn(product):
    return jnp.bitwise_and(product, 2 * F - 1).astype(jnp.float32) * (math.pi / F)


def kernel(
    wt, offs, keep, dist,
    lin_out, ph_out, bin_out,
    j0, j1, j2, j3, far_offs, j32, power_m, power_o, member, ea, eb, table, x, acc,
    s_early, s_late, ra_early, ra_late, pa_early, pa_late, rb, pb, ra2, rb2, g,
    local_sem, send_sem, recv_sem,
):
    joined = (j0, j1, j2, j3)
    chan = lax.axis_index("chan")
    win = lax.axis_index("win")
    core = lax.rem(chan, 2)
    ylo = lax.rem(chan // 2, 2)
    xx = win // 2
    yhi = lax.rem(win, 2)
    above = lax.rem(chan + 4, 32)
    below = lax.rem(chan + 28, 32)
    mate = chan + 1 - 2 * core
    across = chan + 2 - 4 * ylo
    own = ylo * 2 + core
    far = (1 - ylo) * 2 + core
    first_way = jnp.where(ylo == 1, above, below)
    other_way = jnp.where(ylo == 1, below, above)
    early_way = jnp.where(core == 0, below, above)
    late_way = jnp.where(core == 0, above, below)
    early = 2 - core
    late = 3 * core
    owns_early = ylo + core == 1
    owns_late = ylo == core

    x_peer = [lax.rem(xx + d, 4) for d in (1, 2, 3)]
    x_dev = [{"chan": chan, "win": p * 2 + yhi} for p in x_peer]
    y_dev = [
        {"chan": chan, "win": win + 1 - 2 * yhi},
        {"chan": across, "win": win},
        {"chan": across, "win": win + 1 - 2 * yhi},
    ]
    y_half = [1 - yhi, yhi, 1 - yhi]
    far_x = [{"chan": chan, "win": p * 2 + 1 - yhi} for p in x_peer]
    g_dev = [y_dev[0]] + x_dev + far_x

    barrier = pltpu.get_barrier_semaphore()
    greet = [{"chan": c, "win": win} for c in (above, below, mate)] + y_dev + x_dev + far_x
    for dev in greet:
        pl.semaphore_signal(barrier, inc=1, device_id=dev, device_id_type=MESH)
    pl.semaphore_wait(barrier, len(greet))

    count = [0]
    sent = []

    def make(src, dst, device, when=None):
        i = count[0]
        count[0] += 1
        copy = pltpu.make_async_remote_copy(
            src_ref=src, dst_ref=dst, send_sem=send_sem.at[i], recv_sem=recv_sem.at[i],
            device_id=device, device_id_type=MESH,
        )
        sent.append((when, copy))
        return copy

    def send(*args, **kwargs):
        copy = make(*args, **kwargs)
        copy.start()
        return copy

    def near(c):
        return {"chan": c, "win": win}

    offs_copy = send(offs, far_offs, near(across))
    lanes = [pl.ds(q * L, L) for q in range(Q)]
    stay, cross_y, own_first, mate_own = [], [], [], []
    for q in range(Q):
        mine = wt.at[ylo, lanes[q]]
        copy = pltpu.make_async_copy(mine, joined[q].at[4 + own], local_sem.at[q])
        copy.start()
        stay.append(copy)
        cross_y.append(send(wt.at[1 - ylo, lanes[q]], joined[q].at[4 + own], near(across)))
        own_first.append(send(mine, joined[q].at[8 + core - 6 * ylo], near(first_way)))
        mate_own.append(send(mine, joined[q].at[4 + own], near(mate)))
    for_early = [
        make(joined[q].at[4 + early], joined[q].at[10 - 9 * core], near(early_way)) for q in range(Q)
    ]
    for_late = [
        make(joined[q].at[4 + late], joined[q].at[11 * core], near(late_way)) for q in range(Q)
    ]
    for copy in stay:
        copy.wait()

    @pl.when(owns_early)
    def _():
        for_early[0].start()

    @pl.when(owns_late)
    def _():
        for_late[0].start()

    lag = lax.broadcasted_iota(jnp.int32, (FINE, LAGS), 1) - LAGS // 2
    row = lax.broadcasted_iota(jnp.int32, (FINE, LAGS), 0)
    fine = turn(row * lag)
    eb[0] = jnp.cos(fine) * (1.0 / math.sqrt(F))
    eb[1] = jnp.sin(fine) * (1.0 / math.sqrt(F))
    for half in range(F // FINE // FINE):
        coarse = turn((row + half * FINE) * FINE * lag)
        ea[0, half * FINE:(half + 1) * FINE] = jnp.cos(coarse)
        ea[1, half * FINE:(half + 1) * FINE] = jnp.sin(coarse)

    per = KQ // FINE

    def fill(a, _):
        ca = ea[0, pl.ds(a, 1), :]
        sa = ea[1, pl.ds(a, 1), :]
        q2 = (a // per) * 2
        at = pl.ds(pl.multiple_of(lax.rem(a, per) * FINE, FINE), FINE)
        table[q2, at, :] = (eb[0] * ca - eb[1] * sa).astype(jnp.bfloat16)
        table[q2 + 1, at, :] = (eb[1] * ca + eb[0] * sa).astype(jnp.bfloat16)
        return 0

    far_first, mate_far = [], []
    for q in range(Q):
        cross_y[q].wait_recv()
        mine = joined[q].at[4 + far]
        far_first.append(send(mine, joined[q].at[2 + core + 6 * ylo], near(other_way)))
        mate_far.append(send(mine, joined[q].at[4 + far], near(mate)))
        lax.fori_loop(q * per, (q + 1) * per, fill, 0)

    @pl.when(owns_late)
    def _():
        for_early[0].start()

    for q in range(1, Q):
        for_early[q].start()

    place = chan * CH + lax.broadcasted_iota(jnp.int32, (CH, 1), 0)
    every = lax.broadcasted_iota(jnp.int32, (CH, 32 * CH), 1)
    row_dist = dist[...].astype(jnp.float32)

    def distance(index):
        return jnp.sum(jnp.where(every == index, row_dist, 0.0), axis=1, keepdims=True)

    own_dist = distance(place)
    for k in range(2):
        partner = jnp.bitwise_and(place + offs[0, k], 32 * CH - 1)
        bins = jnp.minimum(jnp.abs(distance(partner) - own_dist), NBIN - 1.0)
        column = lax.broadcasted_iota(jnp.int32, (CH, 128), 1).astype(jnp.float32)
        member[k] = (bins == column).astype(jnp.float32)

    offs_copy.wait_recv()
    forward = []
    for q in range(Q):
        own_first[q].wait_recv()
        far_first[q].wait_recv()
        forward.append([
            send(joined[q].at[pos], joined[q].at[pos], near(mate)) for pos in (2 + core, 8 + core)
        ])

    def widen(q, first, number):
        def one(i, _):
            p = first + i
            at = pl.ds(pl.multiple_of(p * CH, CH), CH)
            for lg in range(L):
                for ri in range(2):
                    j32[(q * L + lg) * 2 + ri, at, :] = joined[q][p, lg, ri].astype(jnp.float32)
            return 0

        lax.fori_loop(0, number, one, 0)

    def correlate(q, h, block, owns):
        at_m = pl.ds(pl.multiple_of((4 + block) * CH, CH), CH)
        for k in range(2):
            at_o = pl.ds((4 + block) * CH + jnp.where(owns, offs[0, k], far_offs[0, k]), CH)
            sum_m, sum_o = None, None
            for lg in range(L):
                j = (q * L + lg) * 2
                mr, mi = j32[j, at_m, :], j32[j + 1, at_m, :]
                orr, oi = j32[j, at_o, :], j32[j + 1, at_o, :]
                square = orr * orr + oi * oi
                sum_o = square if sum_o is None else sum_o + square
                if k == 0:
                    square = mr * mr + mi * mi
                    sum_m = square if sum_m is None else sum_m + square
                mr, mi = mr * LIFT, mi * LIFT
                real = (mr * orr + mi * oi).astype(jnp.bfloat16)
                imag = (mi * orr - mr * oi).astype(jnp.bfloat16)
                top = slice(k * CH, (k + 1) * CH)
                low = slice((2 + k) * CH, (3 + k) * CH)
                one = slice(lg * 128, (lg + 1) * 128)
                two = slice(KQ + lg * 128, KQ + (lg + 1) * 128)
                x[top, one] = real
                x[top, two] = -imag
                x[low, one] = imag
                x[low, two] = real
            power_o[h * 2 + k] = sum_o if q == 0 else power_o[h * 2 + k] + sum_o
            if k == 0:
                power_m[h] = sum_m if q == 0 else power_m[h] + sum_m

        def multiply(n, _):
            at = pl.ds(pl.multiple_of(n * 256, 256), 256)
            value = jnp.dot(x[:, :KQ], table[2 * q, :, at], preferred_element_type=jnp.float32)
            value += jnp.dot(x[:, KQ:], table[2 * q + 1, :, at], preferred_element_type=jnp.float32)
            if q == 0:
                acc[:, at] = value
            else:
                acc[:, at] += value
            return 0

        lax.fori_loop(0, LAGS // 256, multiply, 0)

    weight = jnp.where(ylo == 0, keep[0], keep[1]).astype(jnp.float32)

    def stack(h, s):
        for k in range(2):
            def one(i, _):
                r = k * CH + i * 16
                at = pl.ds(pl.multiple_of(i * 16, 16), 16)
                mean_m = jnp.sum(power_m[h, at, :], axis=1, keepdims=True) * (1.0 / F)
                mean_o = jnp.sum(power_o[h * 2 + k, at, :], axis=1, keepdims=True) * (1.0 / F)
                gain = lax.rsqrt(mean_m + EPS) * (1.0 / LIFT) * lax.rsqrt(mean_o + EPS)
                real = acc[pl.ds(pl.multiple_of(r, 16), 16), :] * gain
                imag = acc[pl.ds(pl.multiple_of(2 * CH + r, 16), 16), :] * gain
                scale = weight * jnp.minimum(lax.rsqrt(real * real + imag * imag), 1.0 / FLOOR)
                s[0, k, at, :] = (weight * real).astype(jnp.bfloat16)
                s[1, k, at, :] = (scale * real).astype(jnp.bfloat16)
                s[2, k, at, :] = (scale * imag).astype(jnp.bfloat16)
                return 0

            lax.fori_loop(0, CH // 16, one, 0)

    def rows16(i):
        return pl.ds(pl.multiple_of(i * 16, 16), 16)

    def rows32(i):
        return pl.ds(pl.multiple_of(i * 32, 32), 32)

    def cols512(i):
        return pl.ds(pl.multiple_of(i * 512, 512), 512)

    def cols256(i):
        return pl.ds(pl.multiple_of(i * 256, 256), 256)

    def to_owners(source, target, owns):
        copies = [
            make(source(y_half[n]), target.at[n], y_dev[n], when=owns if n == 0 else ~owns)
            for n in range(3)
        ]

        @pl.when(owns)
        def _():
            copies[0].start()

        @pl.when(~owns)
        def _():
            copies[1].start()
            copies[2].start()

        return copies

    def first_sums(s, ra, owns):
        a = [send(s.at[:, 0, rows16(x_peer[d]), :], ra.at[d], x_dev[d]) for d in range(3)]
        b = to_owners(lambda half: s.at[:, 1, rows32(half), :], rb, owns)
        return a, b

    def second_sums(s, ra, pa, owns, copies):
        a, b = copies
        for copy in a:
            copy.wait_recv()
        for v in range(3):
            total = s[v, 0, rows16(xx), :].astype(jnp.float32)
            for d in range(3):
                total += ra[d, v].astype(jnp.float32)
            pa[v] = total.astype(jnp.bfloat16)
        a2 = to_owners(lambda half: pa.at[:, :, cols512(half)], ra2, owns)
        b2 = [make(pb.at[:, :, cols256(x_peer[d])], rb2.at[d], x_dev[d], when=owns) for d in range(3)]

        @pl.when(owns)
        def _():
            for copy in b:
                copy.wait_recv()
            for v in range(3):
                total = s[v, 1, rows32(yhi), :].astype(jnp.float32)
                for d in range(3):
                    total += rb[d, v].astype(jnp.float32)
                pb[v] = total.astype(jnp.bfloat16)
            for copy in b2:
                copy.start()

        return a2, b2

    def finish(parts):
        linear = parts[0] * (1.0 / 4.0)
        phased = linear * jnp.sqrt(parts[1] * parts[1] + parts[2] * parts[2]) * (1.0 / 16.0)
        return linear.astype(jnp.bfloat16), phased.astype(jnp.bfloat16)

    piece_a = g.at[:, 0, rows16(xx), cols512(yhi)]
    piece_b = g.at[:, 1, rows32(yhi), cols256(xx)]
    last_a = [make(piece_a, piece_a, dev) for dev in g_dev]
    last_b = [make(piece_b, piece_b, dev) for dev in g_dev]

    def results(pa, owns, copies):
        a2, b2 = copies

        @pl.when(owns)
        def _():
            for copy in a2:
                copy.wait_recv()
            parts = []
            for v in range(3):
                total = pa[v, :, cols512(yhi)].astype(jnp.float32)
                for d in range(3):
                    total += ra2[d, v].astype(jnp.float32)
                parts.append(total)
            linear, phased = finish(parts)
            g[0, 0, rows16(xx), cols512(yhi)] = linear
            g[1, 0, rows16(xx), cols512(yhi)] = phased
            for copy in last_a:
                copy.start()
            for copy in b2:
                copy.wait_recv()
            parts = []
            for v in range(3):
                total = pb[v, :, cols256(xx)].astype(jnp.float32)
                for d in range(3):
                    total += rb2[d, v].astype(jnp.float32)
                parts.append(total)
            linear, phased = finish(parts)
            g[0, 1, rows32(yhi), cols256(xx)] = linear
            g[1, 1, rows32(yhi), cols256(xx)] = phased
            for copy in last_b:
                copy.start()

    pass_on = []
    for q in range(Q):
        mate_own[q].wait_recv()
        mate_far[q].wait_recv()
        for copy in forward[q]:
            copy.wait_recv()
        for_early[q].wait_recv()
        pos = 10 - 9 * core
        pass_on.append(send(joined[q].at[pos], joined[q].at[pos], near(mate)))
        if q == 0:
            @pl.when(owns_early)
            def _():
                for_late[0].start()
        else:
            for_late[q].start()
        widen(q, 2 - core, 9)
        correlate(q, 0, early, owns_early)
    stack(0, s_early)
    early_first = first_sums(s_early, ra_early, owns_early)
    for q in range(Q):
        pass_on[q].wait_recv()
        for_late[q].wait_recv()
        widen(q, 10 * core, 2)
        correlate(q, 1, late, owns_late)
    stack(1, s_late)
    late_first = first_sums(s_late, ra_late, owns_late)
    early_second = second_sums(s_early, ra_early, pa_early, owns_early, early_first)
    late_second = second_sums(s_late, ra_late, pa_late, owns_late, late_first)
    results(pa_early, owns_early, early_second)
    results(pa_late, owns_late, late_second)

    for copy in last_a + last_b:
        copy.wait_recv()
    for k in range(2):
        lin_out[k] = g[0, k].astype(jnp.float32)
        ph_out[k] = g[1, k].astype(jnp.float32)
    bins = jnp.zeros((128, LAGS), jnp.float32)
    for k in range(2):
        bins += lax.dot_general(
            member[k].astype(jnp.bfloat16), g[0, k], (((0,), (0,)), ((), ())),
            preferred_element_type=jnp.float32,
        )
    bin_out[...] = bins[:NBIN]
    for when, copy in sent:
        if when is None:
            copy.wait_send()
        else:
            pl.when(when)(copy.wait_send)


def stacks(wt, offs, keep, dist):
    vmem = pl.BlockSpec(memory_space=pltpu.VMEM)
    smem = pl.BlockSpec(memory_space=pltpu.SMEM)
    bf16, f32 = jnp.bfloat16, jnp.float32
    copies = 1 + 10 * Q + 2 * 12 + 14
    block = (12, L, 2, CH, 128)
    return pl.pallas_call(
        kernel,
        out_shape=(
            jax.ShapeDtypeStruct((2, CH, LAGS), f32),
            jax.ShapeDtypeStruct((2, CH, LAGS), f32),
            jax.ShapeDtypeStruct((NBIN, LAGS), f32),
        ),
        in_specs=[pl.BlockSpec(memory_space=pl.ANY), smem, smem, vmem],
        out_specs=(vmem, vmem, vmem),
        scratch_shapes=[
            *[pltpu.VMEM(block, bf16)] * Q,
            pltpu.SMEM((1, 2), jnp.int32),
            pltpu.VMEM((Q * 2 * L, 12 * CH, 128), f32),
            pltpu.VMEM((2, CH, 128), f32),
            pltpu.VMEM((4, CH, 128), f32),
            pltpu.VMEM((2, CH, 128), f32),
            pltpu.VMEM((2, F // FINE, LAGS), f32),
            pltpu.VMEM((2, FINE, LAGS), f32),
            pltpu.VMEM((2 * Q, KQ, LAGS), bf16),
            pltpu.VMEM((4 * CH, 2 * KQ), bf16),
            pltpu.VMEM((4 * CH, LAGS), f32),
            pltpu.VMEM((3, 2, CH, LAGS), bf16),
            pltpu.VMEM((3, 2, CH, LAGS), bf16),
            pltpu.VMEM((3, 3, 16, LAGS), bf16),
            pltpu.VMEM((3, 3, 16, LAGS), bf16),
            pltpu.VMEM((3, 16, LAGS), bf16),
            pltpu.VMEM((3, 16, LAGS), bf16),
            pltpu.VMEM((3, 3, 32, LAGS), bf16),
            pltpu.VMEM((3, 32, LAGS), bf16),
            pltpu.VMEM((3, 3, 16, 512), bf16),
            pltpu.VMEM((3, 3, 32, 256), bf16),
            pltpu.VMEM((2, 2, CH, LAGS), bf16),
            pltpu.SemaphoreType.DMA((Q,)),
            pltpu.SemaphoreType.DMA((copies,)),
            pltpu.SemaphoreType.DMA((copies,)),
        ],
        compiler_params=pltpu.CompilerParams(
            collective_id=0, has_side_effects=True, vmem_limit_bytes=52 * 1024 * 1024
        ),
    )(wt, offs, keep, dist)


def local(spectra, band_offsets, window_keep, chan_dist):
    win_dev, ch_dev, _, freqs = spectra.shape
    wt = spectra.reshape(win_dev, ch_dev, 2, freqs // 128, 128).transpose(0, 3, 2, 1, 4)
    linear, phased, binned = stacks(wt, band_offsets, window_keep, chan_dist[None, :])
    return (linear.transpose(1, 0, 2), phased.transpose(1, 0, 2), binned)


def solution(mesh):
    in_specs = (P("win", "chan", None, None), P("chan", None), P("win"), P())
    out_specs = (P("chan", None, None), P("chan", None, None), P("chan", None))
    return jax.shard_map(local, mesh=mesh, in_specs=in_specs, out_specs=out_specs, check_vma=False)
```

```python
import functools
import math

import jax
import jax.numpy as jnp
from jax import lax
from jax.experimental import pallas as pl
from jax.experimental.pallas import tpu as pltpu
from jax.sharding import PartitionSpec as P

LAGS = 1024
NBIN = 32
EPS = 1e-06
FLOOR = 0.1

F = 2048
CH = 64
Q = 4
L = F // 128 // Q
KQ = L * 128
FINE = 32
LIFT = 2.0**20
MESH = pl.DeviceIdType.MESH


def turn(product):
    return jnp.bitwise_and(product, 2 * F - 1).astype(jnp.float32) * (math.pi / F)


def kernel(
    wt, offs_in, keep_in, dist_in,
    lin_out, ph_out, bin_out,
    j0, j1, j2, j3, offs, keep, dist, far_offs, j32, power_m, power_o, member, ea, eb, table, x, acc,
    s_early, s_late, ra_early, ra_late, pa_early, pa_late, rb, pb, ra2, rb2, g,
    local_sem, small_sem, send_sem, recv_sem,
):
    joined = (j0, j1, j2, j3)
    chan = lax.axis_index("chan")
    win = lax.axis_index("win")
    core = lax.rem(chan, 2)
    ylo = lax.rem(chan // 2, 2)
    xx = win // 2
    yhi = lax.rem(win, 2)
    above = lax.rem(chan + 4, 32)
    below = lax.rem(chan + 28, 32)
    mate = chan + 1 - 2 * core
    across = chan + 2 - 4 * ylo
    own = ylo * 2 + core
    far = (1 - ylo) * 2 + core
    first_way = jnp.where(ylo == 1, above, below)
    other_way = jnp.where(ylo == 1, below, above)
    early_way = jnp.where(core == 0, below, above)
    late_way = jnp.where(core == 0, above, below)
    early = 2 - core
    late = 3 * core
    owns_early = ylo + core == 1
    owns_late = ylo == core

    x_peer = [lax.rem(xx + d, 4) for d in (1, 2, 3)]
    x_dev = [{"chan": chan, "win": p * 2 + yhi} for p in x_peer]
    y_dev = [
        {"chan": chan, "win": win + 1 - 2 * yhi},
        {"chan": across, "win": win},
        {"chan": across, "win": win + 1 - 2 * yhi},
    ]
    y_half = [1 - yhi, yhi, 1 - yhi]
    far_x = [{"chan": chan, "win": p * 2 + 1 - yhi} for p in x_peer]
    g_dev = [y_dev[0]] + x_dev + far_x

    small = [
        pltpu.make_async_copy(source, target, small_sem.at[n])
        for n, (source, target) in enumerate(((offs_in, offs), (keep_in, keep), (dist_in, dist)))
    ]
    for copy in small:
        copy.start()
    barrier = pltpu.get_barrier_semaphore()
    greet = [{"chan": c, "win": win} for c in (above, below, mate)] + y_dev + x_dev + far_x
    for dev in greet:
        pl.semaphore_signal(barrier, inc=1, device_id=dev, device_id_type=MESH)
    pl.semaphore_wait(barrier, len(greet))

    count = [0]
    sent = []

    def make(src, dst, device, when=None):
        i = count[0]
        count[0] += 1
        copy = pltpu.make_async_remote_copy(
            src_ref=src, dst_ref=dst, send_sem=send_sem.at[i], recv_sem=recv_sem.at[i],
            device_id=device, device_id_type=MESH,
        )
        sent.append((when, copy))
        return copy

    def send(*args, **kwargs):
        copy = make(*args, **kwargs)
        copy.start()
        return copy

    def near(c):
        return {"chan": c, "win": win}

    lanes = [pl.ds(q * KQ, KQ) for q in range(Q)]
    stay, cross_y, own_first, mate_own = [], [], [], []
    for q in range(Q):
        mine = wt.at[ylo, :, :, lanes[q]]
        copy = pltpu.make_async_copy(mine, joined[q].at[4 + own], local_sem.at[q])
        copy.start()
        stay.append(copy)
        cross_y.append(send(wt.at[1 - ylo, :, :, lanes[q]], joined[q].at[4 + own], near(across)))
        own_first.append(send(mine, joined[q].at[8 + core - 6 * ylo], near(first_way)))
        mate_own.append(send(mine, joined[q].at[4 + own], near(mate)))
    for_early = [
        make(joined[q].at[4 + early], joined[q].at[10 - 9 * core], near(early_way)) for q in range(Q)
    ]
    for_late = [
        make(joined[q].at[4 + late], joined[q].at[11 * core], near(late_way)) for q in range(Q)
    ]
    for copy in small + stay:
        copy.wait()
    offs_copy = send(offs, far_offs, near(across))

    @pl.when(owns_early)
    def _():
        for_early[0].start()
        for_early[1].start()

    lag = lax.broadcasted_iota(jnp.int32, (FINE, LAGS), 1) - LAGS // 2
    row = lax.broadcasted_iota(jnp.int32, (FINE, LAGS), 0)
    fine = turn(row * lag)
    eb[0] = jnp.cos(fine) * (1.0 / math.sqrt(F))
    eb[1] = jnp.sin(fine) * (1.0 / math.sqrt(F))
    for half in range(F // FINE // FINE):
        coarse = turn((row + half * FINE) * FINE * lag)
        ea[0, half * FINE:(half + 1) * FINE] = jnp.cos(coarse)
        ea[1, half * FINE:(half + 1) * FINE] = jnp.sin(coarse)

    per = KQ // FINE

    def fill(a, _):
        ca = ea[0, pl.ds(a, 1), :]
        sa = ea[1, pl.ds(a, 1), :]
        q2 = (a // per) * 2
        at = pl.ds(pl.multiple_of(lax.rem(a, per) * FINE, FINE), FINE)
        table[q2, at, :] = (eb[0] * ca - eb[1] * sa).astype(jnp.bfloat16)
        table[q2 + 1, at, :] = (eb[1] * ca + eb[0] * sa).astype(jnp.bfloat16)
        return 0

    far_first, mate_far = [], []
    for q in range(Q):
        cross_y[q].wait_recv()
        mine = joined[q].at[4 + far]
        far_first.append(send(mine, joined[q].at[2 + core + 6 * ylo], near(other_way)))
        mate_far.append(send(mine, joined[q].at[4 + far], near(mate)))
        if q >= 2:
            pl.when(owns_late)(for_early[q - 2].start)
        lax.fori_loop(q * per, (q + 1) * per, fill, 0)

    for q in range(2, Q):
        for_early[q].start()

    place = chan * CH + lax.broadcasted_iota(jnp.int32, (CH, 1), 0)
    every = lax.broadcasted_iota(jnp.int32, (CH, 32 * CH), 1)
    row_dist = dist[...].astype(jnp.float32)

    def distance(index):
        return jnp.sum(jnp.where(every == index, row_dist, 0.0), axis=1, keepdims=True)

    own_dist = distance(place)
    for k in range(2):
        partner = jnp.bitwise_and(place + offs[0, k], 32 * CH - 1)
        bins = jnp.minimum(jnp.abs(distance(partner) - own_dist), NBIN - 1.0)
        column = lax.broadcasted_iota(jnp.int32, (CH, 128), 1).astype(jnp.float32)
        member[k] = (bins == column).astype(jnp.float32)

    offs_copy.wait_recv()
    forward = []
    for q in range(Q):
        own_first[q].wait_recv()
        far_first[q].wait_recv()
        forward.append([
            send(joined[q].at[pos], joined[q].at[pos], near(mate)) for pos in (2 + core, 8 + core)
        ])

    def widen(q, first, number):
        def one(i, _):
            p = first + i
            at = pl.ds(pl.multiple_of(p * CH, CH), CH)
            for lg in range(L):
                for ri in range(2):
                    j32[(q * L + lg) * 2 + ri, at, :] = joined[q][p, ri, :, lg * 128:(lg + 1) * 128].astype(jnp.float32)
            return 0

        lax.fori_loop(0, number, one, 0)

    def correlate(q, h, block, owns):
        at_m = pl.ds(pl.multiple_of((4 + block) * CH, CH), CH)
        for k in range(2):
            at_o = pl.ds((4 + block) * CH + jnp.where(owns, offs[0, k], far_offs[0, k]), CH)
            sum_m, sum_o = None, None
            for lg in range(L):
                j = (q * L + lg) * 2
                mr, mi = j32[j, at_m, :], j32[j + 1, at_m, :]
                orr, oi = j32[j, at_o, :], j32[j + 1, at_o, :]
                square = orr * orr + oi * oi
                sum_o = square if sum_o is None else sum_o + square
                if k == 0:
                    square = mr * mr + mi * mi
                    sum_m = square if sum_m is None else sum_m + square
                mr, mi = mr * LIFT, mi * LIFT
                real = (mr * orr + mi * oi).astype(jnp.bfloat16)
                imag = (mi * orr - mr * oi).astype(jnp.bfloat16)
                top = slice(k * CH, (k + 1) * CH)
                low = slice((2 + k) * CH, (3 + k) * CH)
                one = slice(lg * 128, (lg + 1) * 128)
                two = slice(KQ + lg * 128, KQ + (lg + 1) * 128)
                x[top, one] = real
                x[top, two] = -imag
                x[low, one] = imag
                x[low, two] = real
            power_o[h * 2 + k] = sum_o if q == 0 else power_o[h * 2 + k] + sum_o
            if k == 0:
                power_m[h] = sum_m if q == 0 else power_m[h] + sum_m

        def multiply(n, _):
            at = pl.ds(pl.multiple_of(n * 256, 256), 256)
            value = jnp.dot(x[:, :KQ], table[2 * q, :, at], preferred_element_type=jnp.float32)
            value += jnp.dot(x[:, KQ:], table[2 * q + 1, :, at], preferred_element_type=jnp.float32)
            if q == 0:
                acc[:, at] = value
            else:
                acc[:, at] += value
            return 0

        lax.fori_loop(0, LAGS // 256, multiply, 0)

    weight = jnp.where(ylo == 0, keep[0], keep[1]).astype(jnp.float32)

    def stack(h, s):
        for k in range(2):
            def one(i, _):
                r = k * CH + i * 16
                at = pl.ds(pl.multiple_of(i * 16, 16), 16)
                mean_m = jnp.sum(power_m[h, at, :], axis=1, keepdims=True) * (1.0 / F)
                mean_o = jnp.sum(power_o[h * 2 + k, at, :], axis=1, keepdims=True) * (1.0 / F)
                gain = lax.rsqrt(mean_m + EPS) * (1.0 / LIFT) * lax.rsqrt(mean_o + EPS)
                real = acc[pl.ds(pl.multiple_of(r, 16), 16), :] * gain
                imag = acc[pl.ds(pl.multiple_of(2 * CH + r, 16), 16), :] * gain
                scale = weight * jnp.minimum(lax.rsqrt(real * real + imag * imag), 1.0 / FLOOR)
                s[0, k, at, :] = (weight * real).astype(jnp.bfloat16)
                s[1, k, at, :] = (scale * real).astype(jnp.bfloat16)
                s[2, k, at, :] = (scale * imag).astype(jnp.bfloat16)
                return 0

            lax.fori_loop(0, CH // 16, one, 0)

    def rows16(i):
        return pl.ds(pl.multiple_of(i * 16, 16), 16)

    def rows32(i):
        return pl.ds(pl.multiple_of(i * 32, 32), 32)

    def cols512(i):
        return pl.ds(pl.multiple_of(i * 512, 512), 512)

    def cols256(i):
        return pl.ds(pl.multiple_of(i * 256, 256), 256)

    def to_owners(source, target, owns):
        copies = [
            make(source(y_half[n]), target.at[n], y_dev[n], when=owns if n == 0 else ~owns)
            for n in range(3)
        ]

        @pl.when(owns)
        def _():
            copies[0].start()

        @pl.when(~owns)
        def _():
            copies[1].start()
            copies[2].start()

        return copies

    def first_sums(s, ra, owns):
        a = [send(s.at[:, 0, rows16(x_peer[d]), :], ra.at[d], x_dev[d]) for d in range(3)]
        b = to_owners(lambda half: s.at[:, 1, rows32(half), :], rb, owns)
        return a, b

    def second_sums(s, ra, pa, owns, copies):
        a, b = copies
        for copy in a:
            copy.wait_recv()
        for v in range(3):
            total = s[v, 0, rows16(xx), :].astype(jnp.float32)
            for d in range(3):
                total += ra[d, v].astype(jnp.float32)
            pa[v] = total.astype(jnp.bfloat16)
        a2 = to_owners(lambda half: pa.at[:, :, cols512(half)], ra2, owns)
        b2 = [make(pb.at[:, :, cols256(x_peer[d])], rb2.at[d], x_dev[d], when=owns) for d in range(3)]

        @pl.when(owns)
        def _():
            for copy in b:
                copy.wait_recv()
            for v in range(3):
                total = s[v, 1, rows32(yhi), :].astype(jnp.float32)
                for d in range(3):
                    total += rb[d, v].astype(jnp.float32)
                pb[v] = total.astype(jnp.bfloat16)
            for copy in b2:
                copy.start()

        return a2, b2

    def finish(parts):
        linear = parts[0] * (1.0 / 4.0)
        phased = linear * jnp.sqrt(parts[1] * parts[1] + parts[2] * parts[2]) * (1.0 / 16.0)
        return linear.astype(jnp.bfloat16), phased.astype(jnp.bfloat16)

    piece_a = g.at[:, 0, rows16(xx), cols512(yhi)]
    piece_b = g.at[:, 1, rows32(yhi), cols256(xx)]
    last_a = [make(piece_a, piece_a, dev) for dev in g_dev]
    last_b = [make(piece_b, piece_b, dev) for dev in g_dev]

    def results(pa, owns, copies):
        a2, b2 = copies

        @pl.when(owns)
        def _():
            for copy in a2:
                copy.wait_recv()
            parts = []
            for v in range(3):
                total = pa[v, :, cols512(yhi)].astype(jnp.float32)
                for d in range(3):
                    total += ra2[d, v].astype(jnp.float32)
                parts.append(total)
            linear, phased = finish(parts)
            g[0, 0, rows16(xx), cols512(yhi)] = linear
            g[1, 0, rows16(xx), cols512(yhi)] = phased
            for copy in last_a:
                copy.start()
            for copy in b2:
                copy.wait_recv()
            parts = []
            for v in range(3):
                total = pb[v, :, cols256(xx)].astype(jnp.float32)
                for d in range(3):
                    total += rb2[d, v].astype(jnp.float32)
                parts.append(total)
            linear, phased = finish(parts)
            g[0, 1, rows32(yhi), cols256(xx)] = linear
            g[1, 1, rows32(yhi), cols256(xx)] = phased
            for copy in last_b:
                copy.start()

    pass_on = []
    for q in range(Q):
        mate_own[q].wait_recv()
        mate_far[q].wait_recv()
        for copy in forward[q]:
            copy.wait_recv()
        for_early[q].wait_recv()
        pos = 10 - 9 * core
        pass_on.append(send(joined[q].at[pos], joined[q].at[pos], near(mate)))
        for_late[q].start()
        widen(q, 2 - core, 9)
        correlate(q, 0, early, owns_early)
    stack(0, s_early)
    early_first = first_sums(s_early, ra_early, owns_early)
    for q in range(Q):
        pass_on[q].wait_recv()
        for_late[q].wait_recv()
        widen(q, 10 * core, 2)
        correlate(q, 1, late, owns_late)
    stack(1, s_late)
    late_first = first_sums(s_late, ra_late, owns_late)
    early_second = second_sums(s_early, ra_early, pa_early, owns_early, early_first)
    late_second = second_sums(s_late, ra_late, pa_late, owns_late, late_first)
    results(pa_early, owns_early, early_second)
    results(pa_late, owns_late, late_second)

    for copy in last_a + last_b:
        copy.wait_recv()
    for k in range(2):
        lin_out[:, k, :] = g[0, k].astype(jnp.float32)
        ph_out[:, k, :] = g[1, k].astype(jnp.float32)
    bins = jnp.zeros((128, LAGS), jnp.float32)
    for k in range(2):
        bins += lax.dot_general(
            member[k].astype(jnp.bfloat16), g[0, k], (((0,), (0,)), ((), ())),
            preferred_element_type=jnp.float32,
        )
    bin_out[...] = bins[:NBIN]
    for when, copy in sent:
        if when is None:
            copy.wait_send()
        else:
            pl.when(when)(copy.wait_send)


def stacks(wt, offs, keep, dist):
    vmem = pl.BlockSpec(memory_space=pltpu.VMEM)
    bf16, f32 = jnp.bfloat16, jnp.float32
    copies = 1 + 10 * Q + 2 * 12 + 14
    block = (12, 2, CH, KQ)
    return pl.pallas_call(
        kernel,
        out_shape=(
            jax.ShapeDtypeStruct((CH, 2, LAGS), f32),
            jax.ShapeDtypeStruct((CH, 2, LAGS), f32),
            jax.ShapeDtypeStruct((NBIN, LAGS), f32),
        ),
        in_specs=[pl.BlockSpec(memory_space=pl.ANY)] * 4,
        out_specs=(vmem, vmem, vmem),
        scratch_shapes=[
            *[pltpu.VMEM(block, bf16)] * Q,
            pltpu.SMEM((1, 2), jnp.int32),
            pltpu.SMEM((2,), jnp.int32),
            pltpu.VMEM((1, 32 * CH), jnp.int32),
            pltpu.SMEM((1, 2), jnp.int32),
            pltpu.VMEM((Q * 2 * L, 12 * CH, 128), f32),
            pltpu.VMEM((2, CH, 128), f32),
            pltpu.VMEM((4, CH, 128), f32),
            pltpu.VMEM((2, CH, 128), f32),
            pltpu.VMEM((2, F // FINE, LAGS), f32),
            pltpu.VMEM((2, FINE, LAGS), f32),
            pltpu.VMEM((2 * Q, KQ, LAGS), bf16),
            pltpu.VMEM((4 * CH, 2 * KQ), bf16),
            pltpu.VMEM((4 * CH, LAGS), f32),
            pltpu.VMEM((3, 2, CH, LAGS), bf16),
            pltpu.VMEM((3, 2, CH, LAGS), bf16),
            pltpu.VMEM((3, 3, 16, LAGS), bf16),
            pltpu.VMEM((3, 3, 16, LAGS), bf16),
            pltpu.VMEM((3, 16, LAGS), bf16),
            pltpu.VMEM((3, 16, LAGS), bf16),
            pltpu.VMEM((3, 3, 32, LAGS), bf16),
            pltpu.VMEM((3, 32, LAGS), bf16),
            pltpu.VMEM((3, 3, 16, 512), bf16),
            pltpu.VMEM((3, 3, 32, 256), bf16),
            pltpu.VMEM((2, 2, CH, LAGS), bf16),
            pltpu.SemaphoreType.DMA((Q,)),
            pltpu.SemaphoreType.DMA((3,)),
            pltpu.SemaphoreType.DMA((copies,)),
            pltpu.SemaphoreType.DMA((copies,)),
        ],
        compiler_params=pltpu.CompilerParams(
            collective_id=0, has_side_effects=True, vmem_limit_bytes=52 * 1024 * 1024
        ),
    )(wt, offs, keep, dist)


def local(spectra, band_offsets, window_keep, chan_dist):
    win_dev, ch_dev, _, freqs = spectra.shape
    wt = spectra.transpose(0, 2, 1, 3)
    linear, phased, binned = stacks(wt, band_offsets, window_keep, chan_dist[None, :])
    return linear, phased, binned


def solution(mesh):
    in_specs = (P("win", "chan", None, None), P("chan", None), P("win"), P())
    out_specs = (P("chan", None, None), P("chan", None, None), P("chan", None))
    return jax.shard_map(local, mesh=mesh, in_specs=in_specs, out_specs=out_specs, check_vma=False)
```

```python
import functools
import math

import jax
import jax.numpy as jnp
from jax import lax
from jax.experimental import pallas as pl
from jax.experimental.pallas import tpu as pltpu
from jax.sharding import PartitionSpec as P

LAGS = 1024
HALF_LAGS = LAGS // 2
NBIN = 32
EPS = 1e-06
FLOOR = 0.1

F = 2048
CH = 64
Q = 4
L = F // 128 // Q
KQ = L * 128
FINE = 32
LIFT = 2.0**20
MESH = pl.DeviceIdType.MESH


def turn(product):
    return jnp.bitwise_and(product, 4 * F - 1).astype(jnp.float32) * (math.pi / (2 * F))


def kernel(
    wt, offs_in, keep_in, dist_in,
    lin_out, ph_out, bin_out,
    j0, j1, j2, j3, offs, keep, dist, far_offs, j32, power_m, power_o, member, shift, flip, ea, eb, table, x, acc,
    s_early, s_late, ra_early, ra_late, pa_early, pa_late, rb, pb, ra2, rb2, g,
    local_sem, small_sem, send_sem, recv_sem,
):
    joined = (j0, j1, j2, j3)
    chan = lax.axis_index("chan")
    win = lax.axis_index("win")
    core = lax.rem(chan, 2)
    ylo = lax.rem(chan // 2, 2)
    xx = win // 2
    yhi = lax.rem(win, 2)
    above = lax.rem(chan + 4, 32)
    below = lax.rem(chan + 28, 32)
    mate = chan + 1 - 2 * core
    across = chan + 2 - 4 * ylo
    own = ylo * 2 + core
    far = (1 - ylo) * 2 + core
    first_way = jnp.where(ylo == 1, above, below)
    other_way = jnp.where(ylo == 1, below, above)
    early_way = jnp.where(core == 0, below, above)
    late_way = jnp.where(core == 0, above, below)
    early = 2 - core
    late = 3 * core
    owns_early = ylo + core == 1
    owns_late = ylo == core

    x_peer = [lax.rem(xx + d, 4) for d in (1, 2, 3)]
    x_dev = [{"chan": chan, "win": p * 2 + yhi} for p in x_peer]
    y_dev = [
        {"chan": chan, "win": win + 1 - 2 * yhi},
        {"chan": across, "win": win},
        {"chan": across, "win": win + 1 - 2 * yhi},
    ]
    y_half = [1 - yhi, yhi, 1 - yhi]
    far_x = [{"chan": chan, "win": p * 2 + 1 - yhi} for p in x_peer]
    g_dev = [y_dev[0]] + x_dev + far_x

    small = [
        pltpu.make_async_copy(source, target, small_sem.at[n])
        for n, (source, target) in enumerate(((offs_in, offs), (keep_in, keep), (dist_in, dist)))
    ]
    for copy in small:
        copy.start()
    barrier = pltpu.get_barrier_semaphore()
    greet = [{"chan": c, "win": win} for c in (above, below, mate)] + y_dev + x_dev + far_x
    for dev in greet:
        pl.semaphore_signal(barrier, inc=1, device_id=dev, device_id_type=MESH)
    pl.semaphore_wait(barrier, len(greet))

    count = [0]
    sent = []

    def make(src, dst, device, when=None):
        i = count[0]
        count[0] += 1
        copy = pltpu.make_async_remote_copy(
            src_ref=src, dst_ref=dst, send_sem=send_sem.at[i], recv_sem=recv_sem.at[i],
            device_id=device, device_id_type=MESH,
        )
        sent.append((when, copy))
        return copy

    def send(*args, **kwargs):
        copy = make(*args, **kwargs)
        copy.start()
        return copy

    def near(c):
        return {"chan": c, "win": win}

    lanes = [pl.ds(q * KQ, KQ) for q in range(Q)]
    stay, cross_y, own_first, mate_own = [], [], [], []
    for q in range(Q):
        mine = wt.at[ylo, :, :, lanes[q]]
        copy = pltpu.make_async_copy(mine, joined[q].at[4 + own], local_sem.at[q])
        copy.start()
        stay.append(copy)
        cross_y.append(send(wt.at[1 - ylo, :, :, lanes[q]], joined[q].at[4 + own], near(across)))
        own_first.append(send(mine, joined[q].at[8 + core - 6 * ylo], near(first_way)))
        mate_own.append(send(mine, joined[q].at[4 + own], near(mate)))
    for_early = [
        make(joined[q].at[4 + early], joined[q].at[10 - 9 * core], near(early_way)) for q in range(Q)
    ]
    for_late = [
        make(joined[q].at[4 + late], joined[q].at[11 * core], near(late_way)) for q in range(Q)
    ]
    for copy in small + stay:
        copy.wait()
    offs_copy = send(offs, far_offs, near(across))

    @pl.when(owns_early)
    def _():
        for_early[0].start()
        for_early[1].start()

    odd = 2 * lax.broadcasted_iota(jnp.int32, (FINE, HALF_LAGS), 1) + 1
    row = lax.broadcasted_iota(jnp.int32, (FINE, HALF_LAGS), 0)
    fine = turn(row * odd)
    eb[0] = jnp.cos(fine) * (1.0 / math.sqrt(F))
    eb[1] = jnp.sin(fine) * (1.0 / math.sqrt(F))
    for half in range(F // FINE // FINE):
        coarse = turn((row + half * FINE) * FINE * odd)
        ea[0, half * FINE:(half + 1) * FINE] = jnp.cos(coarse)
        ea[1, half * FINE:(half + 1) * FINE] = jnp.sin(coarse)

    step = lax.broadcasted_iota(jnp.int32, (8, F), 1).astype(jnp.float32) * (math.pi / (2 * F))
    shift[0] = jnp.cos(step) * LIFT
    shift[1] = jnp.sin(step) * LIFT
    down_rows = lax.broadcasted_iota(jnp.int32, (HALF_LAGS, HALF_LAGS), 0)
    along = lax.broadcasted_iota(jnp.int32, (HALF_LAGS, HALF_LAGS), 1)
    flip[...] = (down_rows + along == HALF_LAGS - 1).astype(jnp.float32).astype(jnp.bfloat16)

    per = KQ // FINE

    def fill(a, _):
        ca = ea[0, pl.ds(a, 1), :]
        sa = ea[1, pl.ds(a, 1), :]
        chunk = a // per
        at = pl.ds(pl.multiple_of(lax.rem(a, per) * FINE, FINE), FINE)
        table[chunk, at, :HALF_LAGS] = (eb[0] * ca - eb[1] * sa).astype(jnp.bfloat16)
        table[chunk, at, HALF_LAGS:] = (eb[1] * ca + eb[0] * sa).astype(jnp.bfloat16)
        return 0

    far_first, mate_far = [], []
    for q in range(Q):
        cross_y[q].wait_recv()
        mine = joined[q].at[4 + far]
        far_first.append(send(mine, joined[q].at[2 + core + 6 * ylo], near(other_way)))
        mate_far.append(send(mine, joined[q].at[4 + far], near(mate)))
        if q >= 2:
            pl.when(owns_late)(for_early[q - 2].start)
        lax.fori_loop(q * per, (q + 1) * per, fill, 0)

    for q in range(2, Q):
        for_early[q].start()

    place = chan * CH + lax.broadcasted_iota(jnp.int32, (CH, 1), 0)
    every = lax.broadcasted_iota(jnp.int32, (CH, 32 * CH), 1)
    row_dist = dist[...].astype(jnp.float32)

    def distance(index):
        return jnp.sum(jnp.where(every == index, row_dist, 0.0), axis=1, keepdims=True)

    own_dist = distance(place)
    for k in range(2):
        partner = jnp.bitwise_and(place + offs[0, k], 32 * CH - 1)
        bins = jnp.minimum(jnp.abs(distance(partner) - own_dist), NBIN - 1.0)
        column = lax.broadcasted_iota(jnp.int32, (CH, 128), 1).astype(jnp.float32)
        member[k] = (bins == column).astype(jnp.float32)

    offs_copy.wait_recv()
    forward = []
    for q in range(Q):
        own_first[q].wait_recv()
        far_first[q].wait_recv()
        forward.append([
            send(joined[q].at[pos], joined[q].at[pos], near(mate)) for pos in (2 + core, 8 + core)
        ])

    def widen(q, first, number):
        def one(i, _):
            p = first + i
            at = pl.ds(pl.multiple_of(p * CH, CH), CH)
            for lg in range(L):
                for ri in range(2):
                    j32[(q * L + lg) * 2 + ri, at, :] = joined[q][p, ri, :, lg * 128:(lg + 1) * 128].astype(jnp.float32)
            return 0

        lax.fori_loop(0, number, one, 0)

    def correlate(q, h, block, owns):
        at_m = pl.ds(pl.multiple_of((4 + block) * CH, CH), CH)
        at_o = [
            pl.ds((4 + block) * CH + jnp.where(owns, offs[0, k], far_offs[0, k]), CH) for k in range(2)
        ]
        sum_m, sum_o = None, [None, None]
        for lg in range(L):
            j = (q * L + lg) * 2
            mr, mi = j32[j, at_m, :], j32[j + 1, at_m, :]
            square = mr * mr + mi * mi
            sum_m = square if sum_m is None else sum_m + square
            first = (q * L + lg) * 128
            cosine, sine = shift[0, 0:1, first:first + 128], shift[1, 0:1, first:first + 128]
            mr, mi = mr * cosine + mi * sine, mi * cosine - mr * sine
            one = slice(lg * 128, (lg + 1) * 128)
            for k in range(2):
                orr, oi = j32[j, at_o[k], :], j32[j + 1, at_o[k], :]
                square = orr * orr + oi * oi
                sum_o[k] = square if sum_o[k] is None else sum_o[k] + square
                x[k * CH:(k + 1) * CH, one] = (mr * orr + mi * oi).astype(jnp.bfloat16)
                x[(2 + k) * CH:(3 + k) * CH, one] = (mi * orr - mr * oi).astype(jnp.bfloat16)
        power_m[h] = sum_m if q == 0 else power_m[h] + sum_m
        for k in range(2):
            power_o[h * 2 + k] = sum_o[k] if q == 0 else power_o[h * 2 + k] + sum_o[k]

        def multiply(n, _):
            at = pl.ds(pl.multiple_of(n * 256, 256), 256)
            value = jnp.dot(x[...], table[q, :, at], preferred_element_type=jnp.float32)
            if q == 0:
                acc[:, at] = value
            else:
                acc[:, at] += value
            return 0

        lax.fori_loop(0, LAGS // 256, multiply, 0)

    weight = jnp.where(ylo == 0, keep[0], keep[1]).astype(jnp.float32)

    def stack(h, s):
        for k in range(2):
            def one(i, _):
                r = k * CH + i * 16
                at = pl.ds(pl.multiple_of(i * 16, 16), 16)
                mean_m = jnp.sum(power_m[h, at, :], axis=1, keepdims=True) * (1.0 / F)
                mean_o = jnp.sum(power_o[h * 2 + k, at, :], axis=1, keepdims=True) * (1.0 / F)
                gain = lax.rsqrt(mean_m + EPS) * (1.0 / LIFT) * lax.rsqrt(mean_o + EPS)
                even = acc[pl.ds(pl.multiple_of(r, 16), 16), :] * gain
                swap = acc[pl.ds(pl.multiple_of(2 * CH + r, 16), 16), :] * gain
                a, b = even[:, :HALF_LAGS], even[:, HALF_LAGS:]
                c, d = swap[:, :HALF_LAGS], swap[:, HALF_LAGS:]
                real = jnp.concatenate([a + d, a - d], axis=1)
                imag = jnp.concatenate([c - b, c + b], axis=1)
                scale = weight * jnp.minimum(lax.rsqrt(real * real + imag * imag), 1.0 / FLOOR)
                s[0, k, at, :] = (weight * real).astype(jnp.bfloat16)
                s[1, k, at, :] = (scale * real).astype(jnp.bfloat16)
                s[2, k, at, :] = (scale * imag).astype(jnp.bfloat16)
                return 0

            lax.fori_loop(0, CH // 16, one, 0)

    def rows16(i):
        return pl.ds(pl.multiple_of(i * 16, 16), 16)

    def rows32(i):
        return pl.ds(pl.multiple_of(i * 32, 32), 32)

    def cols512(i):
        return pl.ds(pl.multiple_of(i * 512, 512), 512)

    def cols256(i):
        return pl.ds(pl.multiple_of(i * 256, 256), 256)

    def to_owners(source, target, owns):
        copies = [
            make(source(y_half[n]), target.at[n], y_dev[n], when=owns if n == 0 else ~owns)
            for n in range(3)
        ]

        @pl.when(owns)
        def _():
            copies[0].start()

        @pl.when(~owns)
        def _():
            copies[1].start()
            copies[2].start()

        return copies

    def first_sums(s, ra, owns):
        a = [send(s.at[:, 0, rows16(x_peer[d]), :], ra.at[d], x_dev[d]) for d in range(3)]
        b = to_owners(lambda half: s.at[:, 1, rows32(half), :], rb, owns)
        return a, b

    def second_sums(s, ra, pa, owns, copies):
        a, b = copies
        for copy in a:
            copy.wait_recv()
        for v in range(3):
            total = s[v, 0, rows16(xx), :].astype(jnp.float32)
            for d in range(3):
                total += ra[d, v].astype(jnp.float32)
            pa[v] = total.astype(jnp.bfloat16)
        a2 = to_owners(lambda half: pa.at[:, :, cols512(half)], ra2, owns)
        b2 = [make(pb.at[:, :, cols256(x_peer[d])], rb2.at[d], x_dev[d], when=owns) for d in range(3)]

        @pl.when(owns)
        def _():
            for copy in b:
                copy.wait_recv()
            for v in range(3):
                total = s[v, 1, rows32(yhi), :].astype(jnp.float32)
                for d in range(3):
                    total += rb[d, v].astype(jnp.float32)
                pb[v] = total.astype(jnp.bfloat16)
            for copy in b2:
                copy.start()

        return a2, b2

    def finish(parts):
        linear = parts[0] * (1.0 / 4.0)
        phased = linear * jnp.sqrt(parts[1] * parts[1] + parts[2] * parts[2]) * (1.0 / 16.0)
        return linear.astype(jnp.bfloat16), phased.astype(jnp.bfloat16)

    piece_a = g.at[:, 0, rows16(xx), cols512(yhi)]
    piece_b = g.at[:, 1, rows32(yhi), cols256(xx)]
    last_a = [make(piece_a, piece_a, dev) for dev in g_dev]
    last_b = [make(piece_b, piece_b, dev) for dev in g_dev]

    def results(pa, owns, copies):
        a2, b2 = copies

        @pl.when(owns)
        def _():
            for copy in a2:
                copy.wait_recv()
            parts = []
            for v in range(3):
                total = pa[v, :, cols512(yhi)].astype(jnp.float32)
                for d in range(3):
                    total += ra2[d, v].astype(jnp.float32)
                parts.append(total)
            linear, phased = finish(parts)
            g[0, 0, rows16(xx), cols512(yhi)] = linear
            g[1, 0, rows16(xx), cols512(yhi)] = phased
            for copy in last_a:
                copy.start()
            for copy in b2:
                copy.wait_recv()
            parts = []
            for v in range(3):
                total = pb[v, :, cols256(xx)].astype(jnp.float32)
                for d in range(3):
                    total += rb2[d, v].astype(jnp.float32)
                parts.append(total)
            linear, phased = finish(parts)
            g[0, 1, rows32(yhi), cols256(xx)] = linear
            g[1, 1, rows32(yhi), cols256(xx)] = phased
            for copy in last_b:
                copy.start()

    pass_on = []
    for q in range(Q):
        mate_own[q].wait_recv()
        mate_far[q].wait_recv()
        for copy in forward[q]:
            copy.wait_recv()
        widen(q, 2, 8)
        for_early[q].wait_recv()
        pos = 10 - 9 * core
        pass_on.append(send(joined[q].at[pos], joined[q].at[pos], near(mate)))
        for_late[q].start()
        widen(q, 10 - 9 * core, 1)
        correlate(q, 0, early, owns_early)
    stack(0, s_early)
    early_first = first_sums(s_early, ra_early, owns_early)
    for q in range(Q):
        pass_on[q].wait_recv()
        for_late[q].wait_recv()
        widen(q, 10 * core, 2)
        correlate(q, 1, late, owns_late)
    stack(1, s_late)
    late_first = first_sums(s_late, ra_late, owns_late)
    early_second = second_sums(s_early, ra_early, pa_early, owns_early, early_first)
    late_second = second_sums(s_late, ra_late, pa_late, owns_late, late_first)
    results(pa_early, owns_early, early_second)
    results(pa_late, owns_late, late_second)

    for copy in last_a + last_b:
        copy.wait_recv()
    bins_low = jnp.zeros((128, HALF_LAGS), jnp.float32)
    bins_high = jnp.zeros((128, HALF_LAGS), jnp.float32)
    for k in range(2):
        for out, v in ((lin_out, 0), (ph_out, 1)):
            low = jnp.dot(g[v, k, :, :HALF_LAGS], flip[...], preferred_element_type=jnp.float32)
            high = g[v, k, :, HALF_LAGS:]
            out[:, k, :HALF_LAGS] = low
            out[:, k, HALF_LAGS:] = high.astype(jnp.float32)
            if v == 0:
                column = member[k].astype(jnp.bfloat16)
                sides = (((0,), (0,)), ((), ()))
                bins_low += lax.dot_general(
                    column, low.astype(jnp.bfloat16), sides, preferred_element_type=jnp.float32)
                bins_high += lax.dot_general(column, high, sides, preferred_element_type=jnp.float32)
    bin_out[:, :HALF_LAGS] = bins_low[:NBIN]
    bin_out[:, HALF_LAGS:] = bins_high[:NBIN]
    for when, copy in sent:
        if when is None:
            copy.wait_send()
        else:
            pl.when(when)(copy.wait_send)


def stacks(wt, offs, keep, dist):
    vmem = pl.BlockSpec(memory_space=pltpu.VMEM)
    bf16, f32 = jnp.bfloat16, jnp.float32
    copies = 1 + 10 * Q + 2 * 12 + 14
    block = (12, 2, CH, KQ)
    return pl.pallas_call(
        kernel,
        out_shape=(
            jax.ShapeDtypeStruct((CH, 2, LAGS), f32),
            jax.ShapeDtypeStruct((CH, 2, LAGS), f32),
            jax.ShapeDtypeStruct((NBIN, LAGS), f32),
        ),
        in_specs=[pl.BlockSpec(memory_space=pl.ANY)] + [pl.BlockSpec(memory_space=pltpu.HBM)] * 3,
        out_specs=(vmem, vmem, vmem),
        scratch_shapes=[
            *[pltpu.VMEM(block, bf16)] * Q,
            pltpu.SMEM((1, 2), jnp.int32),
            pltpu.SMEM((2,), jnp.int32),
            pltpu.VMEM((1, 32 * CH), jnp.int32),
            pltpu.SMEM((1, 2), jnp.int32),
            pltpu.VMEM((Q * 2 * L, 12 * CH, 128), f32),
            pltpu.VMEM((2, CH, 128), f32),
            pltpu.VMEM((4, CH, 128), f32),
            pltpu.VMEM((2, CH, 128), f32),
            pltpu.VMEM((2, 8, F), f32),
            pltpu.VMEM((HALF_LAGS, HALF_LAGS), bf16),
            pltpu.VMEM((2, F // FINE, HALF_LAGS), f32),
            pltpu.VMEM((2, FINE, HALF_LAGS), f32),
            pltpu.VMEM((Q, KQ, LAGS), bf16),
            pltpu.VMEM((4 * CH, KQ), bf16),
            pltpu.VMEM((4 * CH, LAGS), f32),
            pltpu.VMEM((3, 2, CH, LAGS), bf16),
            pltpu.VMEM((3, 2, CH, LAGS), bf16),
            pltpu.VMEM((3, 3, 16, LAGS), bf16),
            pltpu.VMEM((3, 3, 16, LAGS), bf16),
            pltpu.VMEM((3, 16, LAGS), bf16),
            pltpu.VMEM((3, 16, LAGS), bf16),
            pltpu.VMEM((3, 3, 32, LAGS), bf16),
            pltpu.VMEM((3, 32, LAGS), bf16),
            pltpu.VMEM((3, 3, 16, 512), bf16),
            pltpu.VMEM((3, 3, 32, 256), bf16),
            pltpu.VMEM((2, 2, CH, LAGS), bf16),
            pltpu.SemaphoreType.DMA((Q,)),
            pltpu.SemaphoreType.DMA((3,)),
            pltpu.SemaphoreType.DMA((copies,)),
            pltpu.SemaphoreType.DMA((copies,)),
        ],
        compiler_params=pltpu.CompilerParams(
            collective_id=0, has_side_effects=True, vmem_limit_bytes=52 * 1024 * 1024
        ),
    )(wt, offs, keep, dist)


def local(spectra, band_offsets, window_keep, chan_dist):
    win_dev, ch_dev, _, freqs = spectra.shape
    wt = spectra.transpose(0, 2, 1, 3)
    linear, phased, binned = stacks(wt, band_offsets, window_keep, chan_dist[None, :])
    return linear, phased, binned


def solution(mesh):
    in_specs = (P("win", "chan", None, None), P("chan", None), P("win"), P())
    out_specs = (P("chan", None, None), P("chan", None, None), P("chan", None))
    return jax.shard_map(local, mesh=mesh, in_specs=in_specs, out_specs=out_specs, check_vma=False)
```

```python
import functools
import math

import jax
import jax.numpy as jnp
from jax import lax
from jax.experimental import pallas as pl
from jax.experimental.pallas import tpu as pltpu
from jax.sharding import PartitionSpec as P

LAGS = 1024
HALF_LAGS = LAGS // 2
NBIN = 32
EPS = 1e-06
FLOOR = 0.1

F = 2048
CH = 64
Q = 4
L = F // 128 // Q
KQ = L * 128
FINE = 32
LIFT = 2.0**20
MESH = pl.DeviceIdType.MESH


def turn(product):
    return jnp.bitwise_and(product, 4 * F - 1).astype(jnp.float32) * (math.pi / (2 * F))


def kernel(
    wt, offs_in, keep_in, dist_in,
    lin_out, ph_out, bin_out,
    j0, j1, j2, j3, offs, keep, dist, far_offs, j32, power_m, power_o, member, shift, flip, ea, eb, table, x, acc,
    s_early, s_late, ra_early, ra_late, pa_early, pa_late, rb, pb, ra2, rb2, g,
    local_sem, small_sem, send_sem, recv_sem,
):
    joined = (j0, j1, j2, j3)
    chan = lax.axis_index("chan")
    win = lax.axis_index("win")
    core = lax.rem(chan, 2)
    ylo = lax.rem(chan // 2, 2)
    xx = win // 2
    yhi = lax.rem(win, 2)
    above = lax.rem(chan + 4, 32)
    below = lax.rem(chan + 28, 32)
    mate = chan + 1 - 2 * core
    across = chan + 2 - 4 * ylo
    own = ylo * 2 + core
    far = (1 - ylo) * 2 + core
    first_way = jnp.where(ylo == 1, above, below)
    other_way = jnp.where(ylo == 1, below, above)
    early_way = jnp.where(core == 0, below, above)
    late_way = jnp.where(core == 0, above, below)
    early = 2 - core
    late = 3 * core
    owns_early = ylo + core == 1
    owns_late = ylo == core

    x_peer = [lax.rem(xx + d, 4) for d in (1, 2, 3)]
    x_dev = [{"chan": chan, "win": p * 2 + yhi} for p in x_peer]
    y_dev = [
        {"chan": chan, "win": win + 1 - 2 * yhi},
        {"chan": across, "win": win},
        {"chan": across, "win": win + 1 - 2 * yhi},
    ]
    y_half = [1 - yhi, yhi, 1 - yhi]
    far_x = [{"chan": chan, "win": p * 2 + 1 - yhi} for p in x_peer]
    g_dev = [far_x[1], far_x[0], far_x[2], x_dev[1], y_dev[0], x_dev[0], x_dev[2]]

    small = [
        pltpu.make_async_copy(source, target, small_sem.at[n])
        for n, (source, target) in enumerate(((offs_in, offs), (keep_in, keep), (dist_in, dist)))
    ]
    for copy in small:
        copy.start()
    barrier = pltpu.get_barrier_semaphore()
    greet = [{"chan": c, "win": win} for c in (above, below, mate)] + y_dev + x_dev + far_x
    for dev in greet:
        pl.semaphore_signal(barrier, inc=1, device_id=dev, device_id_type=MESH)
    pl.semaphore_wait(barrier, len(greet))

    count = [0]
    sent = []

    def make(src, dst, device, when=None):
        i = count[0]
        count[0] += 1
        copy = pltpu.make_async_remote_copy(
            src_ref=src, dst_ref=dst, send_sem=send_sem.at[i], recv_sem=recv_sem.at[i],
            device_id=device, device_id_type=MESH,
        )
        sent.append((when, copy))
        return copy

    def send(*args, **kwargs):
        copy = make(*args, **kwargs)
        copy.start()
        return copy

    def near(c):
        return {"chan": c, "win": win}

    lanes = [pl.ds(q * KQ, KQ) for q in range(Q)]
    stay, cross_y, own_first, mate_own = [], [], [], []
    for q in range(Q):
        mine = wt.at[ylo, :, :, lanes[q]]
        copy = pltpu.make_async_copy(mine, joined[q].at[4 + own], local_sem.at[q])
        copy.start()
        stay.append(copy)
        cross_y.append(send(wt.at[1 - ylo, :, :, lanes[q]], joined[q].at[4 + own], near(across)))
        own_first.append(send(mine, joined[q].at[8 + core - 6 * ylo], near(first_way)))
        mate_own.append(send(mine, joined[q].at[4 + own], near(mate)))
    for_early = [
        make(joined[q].at[4 + early], joined[q].at[10 - 9 * core], near(early_way)) for q in range(Q)
    ]
    for_late = [
        make(joined[q].at[4 + late], joined[q].at[11 * core], near(late_way)) for q in range(Q)
    ]
    for copy in small + stay:
        copy.wait()
    offs_copy = send(offs, far_offs, near(across))

    @pl.when(owns_early)
    def _():
        for_early[0].start()
        for_early[1].start()

    odd = 2 * lax.broadcasted_iota(jnp.int32, (FINE, HALF_LAGS), 1) + 1
    row = lax.broadcasted_iota(jnp.int32, (FINE, HALF_LAGS), 0)
    fine = turn(row * odd)
    eb[0] = jnp.cos(fine) * (1.0 / math.sqrt(F))
    eb[1] = jnp.sin(fine) * (1.0 / math.sqrt(F))
    for half in range(F // FINE // FINE):
        coarse = turn((row + half * FINE) * FINE * odd)
        ea[0, half * FINE:(half + 1) * FINE] = jnp.cos(coarse)
        ea[1, half * FINE:(half + 1) * FINE] = jnp.sin(coarse)

    step = lax.broadcasted_iota(jnp.int32, (8, F), 1).astype(jnp.float32) * (math.pi / (2 * F))
    shift[0] = jnp.cos(step) * LIFT
    shift[1] = jnp.sin(step) * LIFT
    down_rows = lax.broadcasted_iota(jnp.int32, (HALF_LAGS, HALF_LAGS), 0)
    along = lax.broadcasted_iota(jnp.int32, (HALF_LAGS, HALF_LAGS), 1)
    flip[...] = (down_rows + along == HALF_LAGS - 1).astype(jnp.float32).astype(jnp.bfloat16)

    per = KQ // FINE

    def fill(a, _):
        ca = ea[0, pl.ds(a, 1), :]
        sa = ea[1, pl.ds(a, 1), :]
        chunk = a // per
        at = pl.ds(pl.multiple_of(lax.rem(a, per) * FINE, FINE), FINE)
        table[chunk, at, :HALF_LAGS] = (eb[0] * ca - eb[1] * sa).astype(jnp.bfloat16)
        table[chunk, at, HALF_LAGS:] = (eb[1] * ca + eb[0] * sa).astype(jnp.bfloat16)
        return 0

    far_first, mate_far = [], []
    for q in range(Q):
        cross_y[q].wait_recv()
        mine = joined[q].at[4 + far]
        far_first.append(send(mine, joined[q].at[2 + core + 6 * ylo], near(other_way)))
        mate_far.append(send(mine, joined[q].at[4 + far], near(mate)))
        if q >= 2:
            pl.when(owns_late)(for_early[q - 2].start)
        lax.fori_loop(q * per, (q + 1) * per, fill, 0)

    for q in range(2, Q):
        for_early[q].start()

    place = chan * CH + lax.broadcasted_iota(jnp.int32, (CH, 1), 0)
    every = lax.broadcasted_iota(jnp.int32, (CH, 32 * CH), 1)
    row_dist = dist[...].astype(jnp.float32)

    def distance(index):
        return jnp.sum(jnp.where(every == index, row_dist, 0.0), axis=1, keepdims=True)

    own_dist = distance(place)
    for k in range(2):
        partner = jnp.bitwise_and(place + offs[0, k], 32 * CH - 1)
        bins = jnp.minimum(jnp.abs(distance(partner) - own_dist), NBIN - 1.0)
        column = lax.broadcasted_iota(jnp.int32, (CH, 128), 1).astype(jnp.float32)
        member[k] = (bins == column).astype(jnp.float32)

    offs_copy.wait_recv()
    forward = []
    for q in range(Q):
        own_first[q].wait_recv()
        far_first[q].wait_recv()
        forward.append([
            send(joined[q].at[pos], joined[q].at[pos], near(mate)) for pos in (2 + core, 8 + core)
        ])

    def widen(q, first, number):
        def one(i, _):
            p = first + i
            at = pl.ds(pl.multiple_of(p * CH, CH), CH)
            for lg in range(L):
                for ri in range(2):
                    j32[(q * L + lg) * 2 + ri, at, :] = joined[q][p, ri, :, lg * 128:(lg + 1) * 128].astype(jnp.float32)
            return 0

        lax.fori_loop(0, number, one, 0)

    def correlate(q, h, block, owns):
        at_m = pl.ds(pl.multiple_of((4 + block) * CH, CH), CH)
        at_o = [
            pl.ds((4 + block) * CH + jnp.where(owns, offs[0, k], far_offs[0, k]), CH) for k in range(2)
        ]
        sum_m, sum_o = None, [None, None]
        for lg in range(L):
            j = (q * L + lg) * 2
            mr, mi = j32[j, at_m, :], j32[j + 1, at_m, :]
            square = mr * mr + mi * mi
            sum_m = square if sum_m is None else sum_m + square
            first = (q * L + lg) * 128
            cosine, sine = shift[0, 0:1, first:first + 128], shift[1, 0:1, first:first + 128]
            mr, mi = mr * cosine + mi * sine, mi * cosine - mr * sine
            one = slice(lg * 128, (lg + 1) * 128)
            for k in range(2):
                orr, oi = j32[j, at_o[k], :], j32[j + 1, at_o[k], :]
                square = orr * orr + oi * oi
                sum_o[k] = square if sum_o[k] is None else sum_o[k] + square
                x[k * CH:(k + 1) * CH, one] = (mr * orr + mi * oi).astype(jnp.bfloat16)
                x[(2 + k) * CH:(3 + k) * CH, one] = (mi * orr - mr * oi).astype(jnp.bfloat16)
        power_m[h] = sum_m if q == 0 else power_m[h] + sum_m
        for k in range(2):
            power_o[h * 2 + k] = sum_o[k] if q == 0 else power_o[h * 2 + k] + sum_o[k]

        def multiply(n, _):
            at = pl.ds(pl.multiple_of(n * 256, 256), 256)
            value = jnp.dot(x[...], table[q, :, at], preferred_element_type=jnp.float32)
            if q == 0:
                acc[:, at] = value
            else:
                acc[:, at] += value
            return 0

        lax.fori_loop(0, LAGS // 256, multiply, 0)

    weight = jnp.where(ylo == 0, keep[0], keep[1]).astype(jnp.float32)

    def stack(h, s):
        for k in range(2):
            def one(i, _):
                r = k * CH + i * 16
                at = pl.ds(pl.multiple_of(i * 16, 16), 16)
                mean_m = jnp.sum(power_m[h, at, :], axis=1, keepdims=True) * (1.0 / F)
                mean_o = jnp.sum(power_o[h * 2 + k, at, :], axis=1, keepdims=True) * (1.0 / F)
                gain = lax.rsqrt(mean_m + EPS) * (1.0 / LIFT) * lax.rsqrt(mean_o + EPS)
                even = acc[pl.ds(pl.multiple_of(r, 16), 16), :] * gain
                swap = acc[pl.ds(pl.multiple_of(2 * CH + r, 16), 16), :] * gain
                a, b = even[:, :HALF_LAGS], even[:, HALF_LAGS:]
                c, d = swap[:, :HALF_LAGS], swap[:, HALF_LAGS:]
                real = jnp.concatenate([a + d, a - d], axis=1)
                imag = jnp.concatenate([c - b, c + b], axis=1)
                scale = weight * jnp.minimum(lax.rsqrt(real * real + imag * imag), 1.0 / FLOOR)
                s[0, k, at, :] = (weight * real).astype(jnp.bfloat16)
                s[1, k, at, :] = (scale * real).astype(jnp.bfloat16)
                s[2, k, at, :] = (scale * imag).astype(jnp.bfloat16)
                return 0

            lax.fori_loop(0, CH // 16, one, 0)

    def rows16(i):
        return pl.ds(pl.multiple_of(i * 16, 16), 16)

    def rows32(i):
        return pl.ds(pl.multiple_of(i * 32, 32), 32)

    def cols256(i):
        return pl.ds(pl.multiple_of(i * 256, 256), 256)

    def to_owners(source, target, owns):
        copies = [
            make(source(y_half[n]), target.at[n], y_dev[n], when=owns if n == 0 else ~owns)
            for n in range(3)
        ]

        @pl.when(owns)
        def _():
            copies[0].start()

        @pl.when(~owns)
        def _():
            copies[1].start()
            copies[2].start()

        return copies

    def first_sums(s, ra, owns):
        a = [send(s.at[:, 0, rows16(x_peer[d]), :], ra.at[d], x_dev[d]) for d in range(3)]
        b = to_owners(lambda half: s.at[:, 1, rows32(half), :], rb, owns)
        return a, b

    def second_sums(s, ra, pa, owns, copies):
        a, b = copies
        for copy in a:
            copy.wait_recv()
        for v in range(3):
            total = s[v, 0, rows16(xx), :].astype(jnp.float32)
            for d in range(3):
                total += ra[d, v].astype(jnp.float32)
            pa[v] = total.astype(jnp.bfloat16)
        a2 = to_owners(lambda half: pa, ra2, owns)
        b2 = [make(pb.at[:, :, cols256(x_peer[d])], rb2.at[d], x_dev[d], when=owns) for d in range(3)]

        @pl.when(owns)
        def _():
            for copy in b:
                copy.wait_recv()
            for v in range(3):
                total = s[v, 1, rows32(yhi), :].astype(jnp.float32)
                for d in range(3):
                    total += rb[d, v].astype(jnp.float32)
                pb[v] = total.astype(jnp.bfloat16)
            for copy in b2:
                copy.start()

        return a2, b2

    def finish(parts):
        linear = parts[0] * (1.0 / 4.0)
        phased = linear * jnp.sqrt(parts[1] * parts[1] + parts[2] * parts[2]) * (1.0 / 16.0)
        return linear.astype(jnp.bfloat16), phased.astype(jnp.bfloat16)

    piece_a = g.at[:, 0, rows16(xx), :]
    piece_b = g.at[:, 1, rows32(yhi), cols256(xx)]
    last_a = [make(piece_a, piece_a, dev) for dev in x_dev]
    last_b = [make(piece_b, piece_b, dev) for dev in g_dev]

    def results(pa, owns, copies):
        a2, b2 = copies

        @pl.when(owns)
        def _():
            for copy in a2:
                copy.wait_recv()
            parts = []
            for v in range(3):
                total = pa[v].astype(jnp.float32)
                for d in range(3):
                    total += ra2[d, v].astype(jnp.float32)
                parts.append(total)
            linear, phased = finish(parts)
            g[0, 0, rows16(xx), :] = linear
            g[1, 0, rows16(xx), :] = phased
            for copy in last_a:
                copy.start()
            for copy in b2:
                copy.wait_recv()
            parts = []
            for v in range(3):
                total = pb[v, :, cols256(xx)].astype(jnp.float32)
                for d in range(3):
                    total += rb2[d, v].astype(jnp.float32)
                parts.append(total)
            linear, phased = finish(parts)
            g[0, 1, rows32(yhi), cols256(xx)] = linear
            g[1, 1, rows32(yhi), cols256(xx)] = phased
            for copy in last_b:
                copy.start()

    pass_on = []
    for q in range(Q):
        mate_own[q].wait_recv()
        mate_far[q].wait_recv()
        for copy in forward[q]:
            copy.wait_recv()
        widen(q, 2, 8)
        for_early[q].wait_recv()
        pos = 10 - 9 * core
        pass_on.append(send(joined[q].at[pos], joined[q].at[pos], near(mate)))
        for_late[q].start()
        widen(q, 10 - 9 * core, 1)
        correlate(q, 0, early, owns_early)
    stack(0, s_early)
    early_first = first_sums(s_early, ra_early, owns_early)
    for q in range(Q):
        pass_on[q].wait_recv()
        for_late[q].wait_recv()
        widen(q, 10 * core, 2)
        correlate(q, 1, late, owns_late)
    stack(1, s_late)
    late_first = first_sums(s_late, ra_late, owns_late)
    early_second = second_sums(s_early, ra_early, pa_early, owns_early, early_first)
    late_second = second_sums(s_late, ra_late, pa_late, owns_late, late_first)
    results(pa_early, owns_early, early_second)
    results(pa_late, owns_late, late_second)

    bins_low = jnp.zeros((128, HALF_LAGS), jnp.float32)
    bins_high = jnp.zeros((128, HALF_LAGS), jnp.float32)
    for k in range(2):
        for copy in (last_a, last_b)[k]:
            copy.wait_recv()
        for out, v in ((lin_out, 0), (ph_out, 1)):
            low = jnp.dot(g[v, k, :, :HALF_LAGS], flip[...], preferred_element_type=jnp.float32)
            high = g[v, k, :, HALF_LAGS:]
            out[:, k, :HALF_LAGS] = low
            out[:, k, HALF_LAGS:] = high.astype(jnp.float32)
            if v == 0:
                column = member[k].astype(jnp.bfloat16)
                sides = (((0,), (0,)), ((), ()))
                bins_low += lax.dot_general(
                    column, low.astype(jnp.bfloat16), sides, preferred_element_type=jnp.float32)
                bins_high += lax.dot_general(column, high, sides, preferred_element_type=jnp.float32)
    bin_out[:, :HALF_LAGS] = bins_low[:NBIN]
    bin_out[:, HALF_LAGS:] = bins_high[:NBIN]
    for when, copy in sent:
        if when is None:
            copy.wait_send()
        else:
            pl.when(when)(copy.wait_send)


def stacks(wt, offs, keep, dist):
    vmem = pl.BlockSpec(memory_space=pltpu.VMEM)
    bf16, f32 = jnp.bfloat16, jnp.float32
    copies = 1 + 10 * Q + 2 * 12 + 10
    block = (12, 2, CH, KQ)
    return pl.pallas_call(
        kernel,
        out_shape=(
            jax.ShapeDtypeStruct((CH, 2, LAGS), f32),
            jax.ShapeDtypeStruct((CH, 2, LAGS), f32),
            jax.ShapeDtypeStruct((NBIN, LAGS), f32),
        ),
        in_specs=[pl.BlockSpec(memory_space=pl.ANY)] + [pl.BlockSpec(memory_space=pltpu.HBM)] * 3,
        out_specs=(vmem, vmem, vmem),
        scratch_shapes=[
            *[pltpu.VMEM(block, bf16)] * Q,
            pltpu.SMEM((1, 2), jnp.int32),
            pltpu.SMEM((2,), jnp.int32),
            pltpu.VMEM((1, 32 * CH), jnp.int32),
            pltpu.SMEM((1, 2), jnp.int32),
            pltpu.VMEM((Q * 2 * L, 12 * CH, 128), f32),
            pltpu.VMEM((2, CH, 128), f32),
            pltpu.VMEM((4, CH, 128), f32),
            pltpu.VMEM((2, CH, 128), f32),
            pltpu.VMEM((2, 8, F), f32),
            pltpu.VMEM((HALF_LAGS, HALF_LAGS), bf16),
            pltpu.VMEM((2, F // FINE, HALF_LAGS), f32),
            pltpu.VMEM((2, FINE, HALF_LAGS), f32),
            pltpu.VMEM((Q, KQ, LAGS), bf16),
            pltpu.VMEM((4 * CH, KQ), bf16),
            pltpu.VMEM((4 * CH, LAGS), f32),
            pltpu.VMEM((3, 2, CH, LAGS), bf16),
            pltpu.VMEM((3, 2, CH, LAGS), bf16),
            pltpu.VMEM((3, 3, 16, LAGS), bf16),
            pltpu.VMEM((3, 3, 16, LAGS), bf16),
            pltpu.VMEM((3, 16, LAGS), bf16),
            pltpu.VMEM((3, 16, LAGS), bf16),
            pltpu.VMEM((3, 3, 32, LAGS), bf16),
            pltpu.VMEM((3, 32, LAGS), bf16),
            pltpu.VMEM((3, 3, 16, LAGS), bf16),
            pltpu.VMEM((3, 3, 32, 256), bf16),
            pltpu.VMEM((2, 2, CH, LAGS), bf16),
            pltpu.SemaphoreType.DMA((Q,)),
            pltpu.SemaphoreType.DMA((3,)),
            pltpu.SemaphoreType.DMA((copies,)),
            pltpu.SemaphoreType.DMA((copies,)),
        ],
        compiler_params=pltpu.CompilerParams(
            collective_id=0, has_side_effects=True, vmem_limit_bytes=52 * 1024 * 1024
        ),
    )(wt, offs, keep, dist)


def local(spectra, band_offsets, window_keep, chan_dist):
    win_dev, ch_dev, _, freqs = spectra.shape
    wt = spectra.transpose(0, 2, 1, 3)
    linear, phased, binned = stacks(wt, band_offsets, window_keep, chan_dist[None, :])
    return linear, phased, binned


def solution(mesh):
    in_specs = (P("win", "chan", None, None), P("chan", None), P("win"), P())
    out_specs = (P("chan", None, None), P("chan", None, None), P("chan", None))
    return jax.shard_map(local, mesh=mesh, in_specs=in_specs, out_specs=out_specs, check_vma=False)
```

```python
import functools
import math

import jax
import jax.numpy as jnp
from jax import lax
from jax.experimental import pallas as pl
from jax.experimental.pallas import tpu as pltpu
from jax.sharding import PartitionSpec as P

LAGS = 1024
HALF_LAGS = LAGS // 2
NBIN = 32
EPS = 1e-06
FLOOR = 0.1

F = 2048
CH = 64
Q = 4
L = F // 128 // Q
KQ = L * 128
FINE = 32
LIFT = 2.0**20
MESH = pl.DeviceIdType.MESH


def turn(product):
    return jnp.bitwise_and(product, 4 * F - 1).astype(jnp.float32) * (math.pi / (2 * F))


def kernel(
    wt, offs_in, keep_in, dist_in,
    lin_out, ph_out, bin_out,
    j0, j1, j2, j3, offs, keep, dist, far_offs, j32, power_m, power_o, member, shift, flip, ea, eb, table, x, acc,
    s_early, s_late, ra_early, ra_late, pa_early, pa_late, rb, pb, ra2, rb2, g,
    local_sem, small_sem, send_sem, recv_sem,
):
    joined = (j0, j1, j2, j3)
    chan = lax.axis_index("chan")
    win = lax.axis_index("win")
    core = lax.rem(chan, 2)
    ylo = lax.rem(chan // 2, 2)
    xx = win // 2
    yhi = lax.rem(win, 2)
    above = lax.rem(chan + 4, 32)
    below = lax.rem(chan + 28, 32)
    mate = chan + 1 - 2 * core
    across = chan + 2 - 4 * ylo
    own = ylo * 2 + core
    far = (1 - ylo) * 2 + core
    first_way = jnp.where(ylo == 1, above, below)
    other_way = jnp.where(ylo == 1, below, above)
    early_way = jnp.where(core == 0, below, above)
    late_way = jnp.where(core == 0, above, below)
    early = 2 - core
    late = 3 * core
    owns_early = ylo + core == 1
    owns_late = ylo == core

    x_peer = [lax.rem(xx + d, 4) for d in (1, 2, 3)]
    x_dev = [{"chan": chan, "win": p * 2 + yhi} for p in x_peer]
    y_dev = [
        {"chan": chan, "win": win + 1 - 2 * yhi},
        {"chan": across, "win": win},
        {"chan": across, "win": win + 1 - 2 * yhi},
    ]
    y_half = [1 - yhi, yhi, 1 - yhi]
    far_x = [{"chan": chan, "win": p * 2 + 1 - yhi} for p in x_peer]
    g_dev = [far_x[1], far_x[0], far_x[2], x_dev[1], y_dev[0], x_dev[0], x_dev[2]]

    small = [
        pltpu.make_async_copy(source, target, small_sem.at[n])
        for n, (source, target) in enumerate(((offs_in, offs), (keep_in, keep), (dist_in, dist)))
    ]
    for copy in small:
        copy.start()
    barrier = pltpu.get_barrier_semaphore()
    greet = [{"chan": c, "win": win} for c in (above, below, mate)] + y_dev + x_dev + far_x
    for dev in greet:
        pl.semaphore_signal(barrier, inc=1, device_id=dev, device_id_type=MESH)
    pl.semaphore_wait(barrier, len(greet))

    count = [0]
    sent = []

    def make(src, dst, device, when=None):
        i = count[0]
        count[0] += 1
        copy = pltpu.make_async_remote_copy(
            src_ref=src, dst_ref=dst, send_sem=send_sem.at[i], recv_sem=recv_sem.at[i],
            device_id=device, device_id_type=MESH,
        )
        sent.append((when, copy))
        return copy

    def send(*args, **kwargs):
        copy = make(*args, **kwargs)
        copy.start()
        return copy

    def near(c):
        return {"chan": c, "win": win}

    lanes = [pl.ds(q * KQ, KQ) for q in range(Q)]
    stay, cross_y, own_first, mate_own = [], [], [], []
    for q in range(Q):
        mine = wt.at[ylo, :, :, lanes[q]]
        copy = pltpu.make_async_copy(mine, joined[q].at[4 + own], local_sem.at[q])
        copy.start()
        stay.append(copy)
        cross_y.append(send(wt.at[1 - ylo, :, :, lanes[q]], joined[q].at[4 + own], near(across)))
        own_first.append(send(mine, joined[q].at[8 + core - 6 * ylo], near(first_way)))
        mate_own.append(send(mine, joined[q].at[4 + own], near(mate)))
    for_early = [
        make(joined[q].at[4 + early], joined[q].at[10 - 9 * core], near(early_way)) for q in range(Q)
    ]
    for_late = [
        make(joined[q].at[4 + late], joined[q].at[11 * core], near(late_way)) for q in range(Q)
    ]
    for copy in small + stay:
        copy.wait()
    offs_copy = send(offs, far_offs, near(across))

    @pl.when(owns_early)
    def _():
        for_early[0].start()
        for_early[1].start()

    odd = 2 * lax.broadcasted_iota(jnp.int32, (FINE, HALF_LAGS), 1) + 1
    row = lax.broadcasted_iota(jnp.int32, (FINE, HALF_LAGS), 0)
    fine = turn(row * odd)
    eb[0] = jnp.cos(fine) * (1.0 / math.sqrt(F))
    eb[1] = jnp.sin(fine) * (1.0 / math.sqrt(F))
    for half in range(F // FINE // FINE):
        coarse = turn((row + half * FINE) * FINE * odd)
        ea[0, half * FINE:(half + 1) * FINE] = jnp.cos(coarse)
        ea[1, half * FINE:(half + 1) * FINE] = jnp.sin(coarse)

    step = lax.broadcasted_iota(jnp.int32, (8, F), 1).astype(jnp.float32) * (math.pi / (2 * F))
    shift[0] = jnp.cos(step) * LIFT
    shift[1] = jnp.sin(step) * LIFT
    down_rows = lax.broadcasted_iota(jnp.int32, (HALF_LAGS, HALF_LAGS), 0)
    along = lax.broadcasted_iota(jnp.int32, (HALF_LAGS, HALF_LAGS), 1)
    flip[...] = (down_rows + along == HALF_LAGS - 1).astype(jnp.float32).astype(jnp.bfloat16)

    per = KQ // FINE

    def fill(a, _):
        ca = ea[0, pl.ds(a, 1), :]
        sa = ea[1, pl.ds(a, 1), :]
        chunk = a // per
        at = pl.ds(pl.multiple_of(lax.rem(a, per) * FINE, FINE), FINE)
        table[chunk, at, :HALF_LAGS] = (eb[0] * ca - eb[1] * sa).astype(jnp.bfloat16)
        table[chunk, at, HALF_LAGS:] = (eb[1] * ca + eb[0] * sa).astype(jnp.bfloat16)
        return 0

    far_first, mate_far = [], []
    for q in range(Q):
        cross_y[q].wait_recv()
        mine = joined[q].at[4 + far]
        far_first.append(send(mine, joined[q].at[2 + core + 6 * ylo], near(other_way)))
        mate_far.append(send(mine, joined[q].at[4 + far], near(mate)))
        if q >= 2:
            pl.when(owns_late)(for_early[q - 2].start)
        lax.fori_loop(q * per, (q + 1) * per, fill, 0)

    for q in range(2, Q):
        for_early[q].start()

    place = chan * CH + lax.broadcasted_iota(jnp.int32, (CH, 1), 0)
    every = lax.broadcasted_iota(jnp.int32, (CH, 32 * CH), 1)
    row_dist = dist[...].astype(jnp.float32)

    def distance(index):
        return jnp.sum(jnp.where(every == index, row_dist, 0.0), axis=1, keepdims=True)

    own_dist = distance(place)
    for k in range(2):
        partner = jnp.bitwise_and(place + offs[0, k], 32 * CH - 1)
        bins = jnp.minimum(jnp.abs(distance(partner) - own_dist), NBIN - 1.0)
        column = lax.broadcasted_iota(jnp.int32, (CH, 128), 1).astype(jnp.float32)
        member[k] = (bins == column).astype(jnp.float32)

    offs_copy.wait_recv()
    forward = []
    for q in range(Q):
        own_first[q].wait_recv()
        far_first[q].wait_recv()
        forward.append([
            send(joined[q].at[pos], joined[q].at[pos], near(mate)) for pos in (2 + core, 8 + core)
        ])

    def widen(q, first, number):
        def one(i, _):
            p = first + i
            at = pl.ds(pl.multiple_of(p * CH, CH), CH)
            for lg in range(L):
                for ri in range(2):
                    j32[(q * L + lg) * 2 + ri, at, :] = joined[q][p, ri, :, lg * 128:(lg + 1) * 128].astype(jnp.float32)
            return 0

        lax.fori_loop(0, number, one, 0)

    def correlate(q, h, block, owns):
        at_m = pl.ds(pl.multiple_of((4 + block) * CH, CH), CH)
        at_o = [
            pl.ds((4 + block) * CH + jnp.where(owns, offs[0, k], far_offs[0, k]), CH) for k in range(2)
        ]
        sum_m, sum_o = None, [None, None]
        for lg in range(L):
            j = (q * L + lg) * 2
            mr, mi = j32[j, at_m, :], j32[j + 1, at_m, :]
            square = mr * mr + mi * mi
            sum_m = square if sum_m is None else sum_m + square
            first = (q * L + lg) * 128
            cosine, sine = shift[0, 0:1, first:first + 128], shift[1, 0:1, first:first + 128]
            mr, mi = mr * cosine + mi * sine, mi * cosine - mr * sine
            one = slice(lg * 128, (lg + 1) * 128)
            for k in range(2):
                orr, oi = j32[j, at_o[k], :], j32[j + 1, at_o[k], :]
                square = orr * orr + oi * oi
                sum_o[k] = square if sum_o[k] is None else sum_o[k] + square
                x[k * CH:(k + 1) * CH, one] = (mr * orr + mi * oi).astype(jnp.bfloat16)
                x[(2 + k) * CH:(3 + k) * CH, one] = (mi * orr - mr * oi).astype(jnp.bfloat16)
        power_m[h] = sum_m if q == 0 else power_m[h] + sum_m
        for k in range(2):
            power_o[h * 2 + k] = sum_o[k] if q == 0 else power_o[h * 2 + k] + sum_o[k]

        def multiply(n, _):
            at = pl.ds(pl.multiple_of(n * 512, 512), 512)
            value = jnp.dot(x[...], table[q, :, at], preferred_element_type=jnp.float32)
            if q == 0:
                acc[:, at] = value
            else:
                acc[:, at] += value
            return 0

        lax.fori_loop(0, LAGS // 512, multiply, 0)

    weight = jnp.where(ylo == 0, keep[0], keep[1]).astype(jnp.float32)

    def stack(h, s, k):
        def one(i, _):
            r = k * CH + i * 16
            at = pl.ds(pl.multiple_of(i * 16, 16), 16)
            mean_m = jnp.sum(power_m[h, at, :], axis=1, keepdims=True) * (1.0 / F)
            mean_o = jnp.sum(power_o[h * 2 + k, at, :], axis=1, keepdims=True) * (1.0 / F)
            gain = lax.rsqrt(mean_m + EPS) * (1.0 / LIFT) * lax.rsqrt(mean_o + EPS)
            even = acc[pl.ds(pl.multiple_of(r, 16), 16), :] * gain
            swap = acc[pl.ds(pl.multiple_of(2 * CH + r, 16), 16), :] * gain
            a, b = even[:, :HALF_LAGS], even[:, HALF_LAGS:]
            c, d = swap[:, :HALF_LAGS], swap[:, HALF_LAGS:]
            real = jnp.concatenate([a + d, a - d], axis=1)
            imag = jnp.concatenate([c - b, c + b], axis=1)
            scale = weight * jnp.minimum(lax.rsqrt(real * real + imag * imag), 1.0 / FLOOR)
            s[0, k, at, :] = (weight * real).astype(jnp.bfloat16)
            s[1, k, at, :] = (scale * real).astype(jnp.bfloat16)
            s[2, k, at, :] = (scale * imag).astype(jnp.bfloat16)
            return 0

        lax.fori_loop(0, CH // 16, one, 0)

    def rows16(i):
        return pl.ds(pl.multiple_of(i * 16, 16), 16)

    def rows32(i):
        return pl.ds(pl.multiple_of(i * 32, 32), 32)

    def cols256(i):
        return pl.ds(pl.multiple_of(i * 256, 256), 256)

    def to_owners(source, target, owns):
        copies = [
            make(source(y_half[n]), target.at[n], y_dev[n], when=owns if n == 0 else ~owns)
            for n in range(3)
        ]

        @pl.when(owns)
        def _():
            copies[0].start()

        @pl.when(~owns)
        def _():
            copies[1].start()
            copies[2].start()

        return copies

    def first_sums(h, s, ra, owns):
        stack(h, s, 1)
        b = to_owners(lambda half: s.at[:, 1, rows32(half), :], rb, owns)
        stack(h, s, 0)
        a = {d: send(s.at[:, 0, rows16(x_peer[d]), :], ra.at[d], x_dev[d]) for d in (1, 0, 2)}
        return list(a.values()), b

    def second_sums(s, ra, pa, owns, copies):
        a, b = copies
        for copy in a:
            copy.wait_recv()
        for v in range(3):
            total = s[v, 0, rows16(xx), :].astype(jnp.float32)
            for d in range(3):
                total += ra[d, v].astype(jnp.float32)
            pa[v] = total.astype(jnp.bfloat16)
        a2 = to_owners(lambda half: pa, ra2, owns)
        b2 = [make(pb.at[:, :, cols256(x_peer[d])], rb2.at[d], x_dev[d], when=owns) for d in range(3)]

        @pl.when(owns)
        def _():
            for copy in b:
                copy.wait_recv()
            for v in range(3):
                total = s[v, 1, rows32(yhi), :].astype(jnp.float32)
                for d in range(3):
                    total += rb[d, v].astype(jnp.float32)
                pb[v] = total.astype(jnp.bfloat16)
            for copy in b2:
                copy.start()

        return a2, b2

    def finish(parts):
        linear = parts[0] * (1.0 / 4.0)
        phased = linear * jnp.sqrt(parts[1] * parts[1] + parts[2] * parts[2]) * (1.0 / 16.0)
        return linear.astype(jnp.bfloat16), phased.astype(jnp.bfloat16)

    piece_a = g.at[:, 0, rows16(xx), :]
    piece_b = g.at[:, 1, rows32(yhi), cols256(xx)]
    last_a = [make(piece_a, piece_a, dev) for dev in x_dev]
    last_b = [make(piece_b, piece_b, dev) for dev in g_dev]

    def results(pa, owns, copies):
        a2, b2 = copies

        @pl.when(owns)
        def _():
            for copy in a2:
                copy.wait_recv()
            parts = []
            for v in range(3):
                total = pa[v].astype(jnp.float32)
                for d in range(3):
                    total += ra2[d, v].astype(jnp.float32)
                parts.append(total)
            linear, phased = finish(parts)
            g[0, 0, rows16(xx), :] = linear
            g[1, 0, rows16(xx), :] = phased
            for copy in last_a:
                copy.start()
            for copy in b2:
                copy.wait_recv()
            parts = []
            for v in range(3):
                total = pb[v, :, cols256(xx)].astype(jnp.float32)
                for d in range(3):
                    total += rb2[d, v].astype(jnp.float32)
                parts.append(total)
            linear, phased = finish(parts)
            g[0, 1, rows32(yhi), cols256(xx)] = linear
            g[1, 1, rows32(yhi), cols256(xx)] = phased
            for copy in last_b:
                copy.start()

    pass_on = []
    for q in range(Q):
        mate_own[q].wait_recv()
        mate_far[q].wait_recv()
        for copy in forward[q]:
            copy.wait_recv()
        widen(q, 2, 8)
        for_early[q].wait_recv()
        pos = 10 - 9 * core
        pass_on.append(send(joined[q].at[pos], joined[q].at[pos], near(mate)))
        for_late[q].start()
        widen(q, 10 - 9 * core, 1)
        correlate(q, 0, early, owns_early)
    early_first = first_sums(0, s_early, ra_early, owns_early)
    for q in range(Q):
        pass_on[q].wait_recv()
        for_late[q].wait_recv()
        widen(q, 10 * core, 2)
        correlate(q, 1, late, owns_late)
    late_first = first_sums(1, s_late, ra_late, owns_late)
    early_second = second_sums(s_early, ra_early, pa_early, owns_early, early_first)
    late_second = second_sums(s_late, ra_late, pa_late, owns_late, late_first)
    results(pa_early, owns_early, early_second)
    results(pa_late, owns_late, late_second)

    bins_low = jnp.zeros((128, HALF_LAGS), jnp.float32)
    bins_high = jnp.zeros((128, HALF_LAGS), jnp.float32)
    for k in range(2):
        for copy in (last_a, last_b)[k]:
            copy.wait_recv()
        for out, v in ((lin_out, 0), (ph_out, 1)):
            low = jnp.dot(g[v, k, :, :HALF_LAGS], flip[...], preferred_element_type=jnp.float32)
            high = g[v, k, :, HALF_LAGS:]
            out[:, k, :HALF_LAGS] = low
            out[:, k, HALF_LAGS:] = high.astype(jnp.float32)
            if v == 0:
                column = member[k].astype(jnp.bfloat16)
                sides = (((0,), (0,)), ((), ()))
                bins_low += lax.dot_general(
                    column, low.astype(jnp.bfloat16), sides, preferred_element_type=jnp.float32)
                bins_high += lax.dot_general(column, high, sides, preferred_element_type=jnp.float32)
    bin_out[:, :HALF_LAGS] = bins_low[:NBIN]
    bin_out[:, HALF_LAGS:] = bins_high[:NBIN]
    for when, copy in sent:
        if when is None:
            copy.wait_send()
        else:
            pl.when(when)(copy.wait_send)


def stacks(wt, offs, keep, dist):
    vmem = pl.BlockSpec(memory_space=pltpu.VMEM)
    bf16, f32 = jnp.bfloat16, jnp.float32
    copies = 1 + 10 * Q + 2 * 12 + 10
    block = (12, 2, CH, KQ)
    return pl.pallas_call(
        kernel,
        out_shape=(
            jax.ShapeDtypeStruct((CH, 2, LAGS), f32),
            jax.ShapeDtypeStruct((CH, 2, LAGS), f32),
            jax.ShapeDtypeStruct((NBIN, LAGS), f32),
        ),
        in_specs=[pl.BlockSpec(memory_space=pl.ANY)] + [pl.BlockSpec(memory_space=pltpu.HBM)] * 3,
        out_specs=(vmem, vmem, vmem),
        scratch_shapes=[
            *[pltpu.VMEM(block, bf16)] * Q,
            pltpu.SMEM((1, 2), jnp.int32),
            pltpu.SMEM((2,), jnp.int32),
            pltpu.VMEM((1, 32 * CH), jnp.int32),
            pltpu.SMEM((1, 2), jnp.int32),
            pltpu.VMEM((Q * 2 * L, 12 * CH, 128), f32),
            pltpu.VMEM((2, CH, 128), f32),
            pltpu.VMEM((4, CH, 128), f32),
            pltpu.VMEM((2, CH, 128), f32),
            pltpu.VMEM((2, 8, F), f32),
            pltpu.VMEM((HALF_LAGS, HALF_LAGS), bf16),
            pltpu.VMEM((2, F // FINE, HALF_LAGS), f32),
            pltpu.VMEM((2, FINE, HALF_LAGS), f32),
            pltpu.VMEM((Q, KQ, LAGS), bf16),
            pltpu.VMEM((4 * CH, KQ), bf16),
            pltpu.VMEM((4 * CH, LAGS), f32),
            pltpu.VMEM((3, 2, CH, LAGS), bf16),
            pltpu.VMEM((3, 2, CH, LAGS), bf16),
            pltpu.VMEM((3, 3, 16, LAGS), bf16),
            pltpu.VMEM((3, 3, 16, LAGS), bf16),
            pltpu.VMEM((3, 16, LAGS), bf16),
            pltpu.VMEM((3, 16, LAGS), bf16),
            pltpu.VMEM((3, 3, 32, LAGS), bf16),
            pltpu.VMEM((3, 32, LAGS), bf16),
            pltpu.VMEM((3, 3, 16, LAGS), bf16),
            pltpu.VMEM((3, 3, 32, 256), bf16),
            pltpu.VMEM((2, 2, CH, LAGS), bf16),
            pltpu.SemaphoreType.DMA((Q,)),
            pltpu.SemaphoreType.DMA((3,)),
            pltpu.SemaphoreType.DMA((copies,)),
            pltpu.SemaphoreType.DMA((copies,)),
        ],
        compiler_params=pltpu.CompilerParams(
            collective_id=0, has_side_effects=True, vmem_limit_bytes=52 * 1024 * 1024
        ),
    )(wt, offs, keep, dist)


def local(spectra, band_offsets, window_keep, chan_dist):
    win_dev, ch_dev, _, freqs = spectra.shape
    wt = spectra.transpose(0, 2, 1, 3)
    linear, phased, binned = stacks(wt, band_offsets, window_keep, chan_dist[None, :])
    return linear, phased, binned


def solution(mesh):
    in_specs = (P("win", "chan", None, None), P("chan", None), P("win"), P())
    out_specs = (P("chan", None, None), P("chan", None, None), P("chan", None))
    return jax.shard_map(local, mesh=mesh, in_specs=in_specs, out_specs=out_specs, check_vma=False)
```

```python
import functools
import math

import jax
import jax.numpy as jnp
from jax import lax
from jax.experimental import pallas as pl
from jax.experimental.pallas import tpu as pltpu
from jax.sharding import PartitionSpec as P

LAGS = 1024
HALF_LAGS = LAGS // 2
NBIN = 32
EPS = 1e-06
FLOOR = 0.1

F = 2048
CH = 64
Q = 4
L = F // 128 // Q
KQ = L * 128
FINE = 32
LIFT = 2.0**20
MESH = pl.DeviceIdType.MESH


def turn(product):
    return jnp.bitwise_and(product, 4 * F - 1).astype(jnp.float32) * (math.pi / (2 * F))


def kernel(
    wt, offs_in, keep_in, dist_in,
    lin_out, ph_out, bin_out,
    j0, j1, j2, j3, offs, keep, dist, far_offs, j32, power_m, power_o, member, shift, flip, ea, eb, table, x, acc,
    s_early, s_late, ra_early, ra_late, pa_early, pa_late, rb, pb, ra2, rb2, g,
    local_sem, small_sem, send_sem, recv_sem,
):
    joined = (j0, j1, j2, j3)
    chan = lax.axis_index("chan")
    win = lax.axis_index("win")
    core = lax.rem(chan, 2)
    ylo = lax.rem(chan // 2, 2)
    xx = win // 2
    yhi = lax.rem(win, 2)
    above = lax.rem(chan + 4, 32)
    below = lax.rem(chan + 28, 32)
    mate = chan + 1 - 2 * core
    across = chan + 2 - 4 * ylo
    own = ylo * 2 + core
    far = (1 - ylo) * 2 + core
    first_way = jnp.where(ylo == 1, above, below)
    other_way = jnp.where(ylo == 1, below, above)
    early_way = jnp.where(core == 0, below, above)
    late_way = jnp.where(core == 0, above, below)
    early = 2 - core
    late = 3 * core
    owns_early = ylo + core == 1
    owns_late = ylo == core

    x_peer = [lax.rem(xx + d, 4) for d in (1, 2, 3)]
    x_dev = [{"chan": chan, "win": p * 2 + yhi} for p in x_peer]
    y_dev = [
        {"chan": chan, "win": win + 1 - 2 * yhi},
        {"chan": across, "win": win},
        {"chan": across, "win": win + 1 - 2 * yhi},
    ]
    y_half = [1 - yhi, yhi, 1 - yhi]
    far_x = [{"chan": chan, "win": p * 2 + 1 - yhi} for p in x_peer]
    g_dev = [far_x[1], far_x[0], far_x[2], x_dev[1], y_dev[0], x_dev[0], x_dev[2]]

    small = [
        pltpu.make_async_copy(source, target, small_sem.at[n])
        for n, (source, target) in enumerate(((offs_in, offs), (keep_in, keep), (dist_in, dist)))
    ]
    for copy in small:
        copy.start()
    barrier = pltpu.get_barrier_semaphore()
    greet = [{"chan": c, "win": win} for c in (above, below, mate)] + y_dev + x_dev + far_x
    for dev in greet:
        pl.semaphore_signal(barrier, inc=1, device_id=dev, device_id_type=MESH)
    pl.semaphore_wait(barrier, len(greet))

    count = [0]
    sent = []

    def make(src, dst, device, when=None):
        i = count[0]
        count[0] += 1
        copy = pltpu.make_async_remote_copy(
            src_ref=src, dst_ref=dst, send_sem=send_sem.at[i], recv_sem=recv_sem.at[i],
            device_id=device, device_id_type=MESH,
        )
        sent.append((when, copy))
        return copy

    def send(*args, **kwargs):
        copy = make(*args, **kwargs)
        copy.start()
        return copy

    def near(c):
        return {"chan": c, "win": win}

    lanes = [pl.ds(q * KQ, KQ) for q in range(Q)]
    stay, cross_y, own_first, mate_own = [], [], [], []
    for q in range(Q):
        mine = wt.at[ylo, :, :, lanes[q]]
        copy = pltpu.make_async_copy(mine, joined[q].at[4 + own], local_sem.at[q])
        copy.start()
        stay.append(copy)
        cross_y.append(send(wt.at[1 - ylo, :, :, lanes[q]], joined[q].at[4 + own], near(across)))
        own_first.append(send(mine, joined[q].at[8 + core - 6 * ylo], near(first_way)))
        mate_own.append(send(mine, joined[q].at[4 + own], near(mate)))
    for_early = [
        make(joined[q].at[4 + early], joined[q].at[10 - 9 * core], near(early_way)) for q in range(Q)
    ]
    for_late = [
        make(joined[q].at[4 + late], joined[q].at[11 * core], near(late_way)) for q in range(Q)
    ]
    for copy in small + stay:
        copy.wait()
    offs_copy = send(offs, far_offs, near(across))

    @pl.when(owns_early)
    def _():
        for_early[0].start()
        for_early[1].start()

    odd = 2 * lax.broadcasted_iota(jnp.int32, (FINE, HALF_LAGS), 1) + 1
    row = lax.broadcasted_iota(jnp.int32, (FINE, HALF_LAGS), 0)
    fine = turn(row * odd)
    eb[0] = jnp.cos(fine) * (1.0 / math.sqrt(F))
    eb[1] = jnp.sin(fine) * (1.0 / math.sqrt(F))
    for half in range(F // FINE // FINE):
        coarse = turn((row + half * FINE) * FINE * odd)
        ea[0, half * FINE:(half + 1) * FINE] = jnp.cos(coarse)
        ea[1, half * FINE:(half + 1) * FINE] = jnp.sin(coarse)

    step = lax.broadcasted_iota(jnp.int32, (8, F), 1).astype(jnp.float32) * (math.pi / (2 * F))
    shift[0] = jnp.cos(step) * LIFT
    shift[1] = jnp.sin(step) * LIFT
    down_rows = lax.broadcasted_iota(jnp.int32, (HALF_LAGS, HALF_LAGS), 0)
    along = lax.broadcasted_iota(jnp.int32, (HALF_LAGS, HALF_LAGS), 1)
    flip[...] = (down_rows + along == HALF_LAGS - 1).astype(jnp.float32).astype(jnp.bfloat16)

    per = KQ // FINE

    def fill(a, _):
        ca = ea[0, pl.ds(a, 1), :]
        sa = ea[1, pl.ds(a, 1), :]
        chunk = a // per
        at = pl.ds(pl.multiple_of(lax.rem(a, per) * FINE, FINE), FINE)
        table[chunk, at, :HALF_LAGS] = (eb[0] * ca - eb[1] * sa).astype(jnp.bfloat16)
        table[chunk, at, HALF_LAGS:] = (eb[1] * ca + eb[0] * sa).astype(jnp.bfloat16)
        return 0

    far_first, mate_far = [], []
    for q in range(Q):
        cross_y[q].wait_recv()
        mine = joined[q].at[4 + far]
        far_first.append(send(mine, joined[q].at[2 + core + 6 * ylo], near(other_way)))
        mate_far.append(send(mine, joined[q].at[4 + far], near(mate)))
        if q >= 2:
            pl.when(owns_late)(for_early[q - 2].start)
        lax.fori_loop(q * per, (q + 1) * per, fill, 0)

    for q in range(2, Q):
        for_early[q].start()

    place = chan * CH + lax.broadcasted_iota(jnp.int32, (CH, 1), 0)
    every = lax.broadcasted_iota(jnp.int32, (CH, 32 * CH), 1)
    row_dist = dist[...].astype(jnp.float32)

    def distance(index):
        return jnp.sum(jnp.where(every == index, row_dist, 0.0), axis=1, keepdims=True)

    own_dist = distance(place)
    for k in range(2):
        partner = jnp.bitwise_and(place + offs[0, k], 32 * CH - 1)
        bins = jnp.minimum(jnp.abs(distance(partner) - own_dist), NBIN - 1.0)
        column = lax.broadcasted_iota(jnp.int32, (CH, 128), 1).astype(jnp.float32)
        member[k] = (bins == column).astype(jnp.float32)

    offs_copy.wait_recv()
    forward = []
    for q in range(Q):
        own_first[q].wait_recv()
        far_first[q].wait_recv()
        forward.append([
            send(joined[q].at[pos], joined[q].at[pos], near(mate)) for pos in (2 + core, 8 + core)
        ])

    def widen(q, first, number):
        def one(i, _):
            p = first + i
            at = pl.ds(pl.multiple_of(p * CH, CH), CH)
            for lg in range(L):
                for ri in range(2):
                    j32[(q * L + lg) * 2 + ri, at, :] = joined[q][p, ri, :, lg * 128:(lg + 1) * 128].astype(jnp.float32)
            return 0

        lax.fori_loop(0, number, one, 0)

    def correlate(q, h, block, owns):
        at_m = pl.ds(pl.multiple_of((4 + block) * CH, CH), CH)
        at_o = [
            pl.ds((4 + block) * CH + jnp.where(owns, offs[0, k], far_offs[0, k]), CH) for k in range(2)
        ]
        sum_m, sum_o = None, [None, None]
        for lg in range(L):
            j = (q * L + lg) * 2
            mr, mi = j32[j, at_m, :], j32[j + 1, at_m, :]
            square = mr * mr + mi * mi
            sum_m = square if sum_m is None else sum_m + square
            first = (q * L + lg) * 128
            cosine, sine = shift[0, 0:1, first:first + 128], shift[1, 0:1, first:first + 128]
            mr, mi = mr * cosine + mi * sine, mi * cosine - mr * sine
            one = slice(lg * 128, (lg + 1) * 128)
            for k in range(2):
                orr, oi = j32[j, at_o[k], :], j32[j + 1, at_o[k], :]
                square = orr * orr + oi * oi
                sum_o[k] = square if sum_o[k] is None else sum_o[k] + square
                x[k * CH:(k + 1) * CH, one] = (mr * orr + mi * oi).astype(jnp.bfloat16)
                x[(2 + k) * CH:(3 + k) * CH, one] = (mi * orr - mr * oi).astype(jnp.bfloat16)
        power_m[h] = sum_m if q == 0 else power_m[h] + sum_m
        for k in range(2):
            power_o[h * 2 + k] = sum_o[k] if q == 0 else power_o[h * 2 + k] + sum_o[k]

        def multiply(n, _):
            at = pl.ds(pl.multiple_of(n * 1024, 1024), 1024)
            value = jnp.dot(x[...], table[q, :, at], preferred_element_type=jnp.float32)
            if q == 0:
                acc[:, at] = value
            else:
                acc[:, at] += value
            return 0

        lax.fori_loop(0, LAGS // 1024, multiply, 0)

    weight = jnp.where(ylo == 0, keep[0], keep[1]).astype(jnp.float32)

    def stack(h, s, k):
        def one(i, _):
            r = k * CH + i * 16
            at = pl.ds(pl.multiple_of(i * 16, 16), 16)
            mean_m = jnp.sum(power_m[h, at, :], axis=1, keepdims=True) * (1.0 / F)
            mean_o = jnp.sum(power_o[h * 2 + k, at, :], axis=1, keepdims=True) * (1.0 / F)
            gain = lax.rsqrt(mean_m + EPS) * (1.0 / LIFT) * lax.rsqrt(mean_o + EPS)
            even = acc[pl.ds(pl.multiple_of(r, 16), 16), :] * gain
            swap = acc[pl.ds(pl.multiple_of(2 * CH + r, 16), 16), :] * gain
            a, b = even[:, :HALF_LAGS], even[:, HALF_LAGS:]
            c, d = swap[:, :HALF_LAGS], swap[:, HALF_LAGS:]
            real = jnp.concatenate([a + d, a - d], axis=1)
            imag = jnp.concatenate([c - b, c + b], axis=1)
            scale = weight * jnp.minimum(lax.rsqrt(real * real + imag * imag), 1.0 / FLOOR)
            s[0, k, at, :] = (weight * real).astype(jnp.bfloat16)
            s[1, k, at, :] = (scale * real).astype(jnp.bfloat16)
            s[2, k, at, :] = (scale * imag).astype(jnp.bfloat16)
            return 0

        lax.fori_loop(0, CH // 16, one, 0)

    def rows16(i):
        return pl.ds(pl.multiple_of(i * 16, 16), 16)

    def rows32(i):
        return pl.ds(pl.multiple_of(i * 32, 32), 32)

    def cols256(i):
        return pl.ds(pl.multiple_of(i * 256, 256), 256)

    def to_owners(source, target, owns):
        copies = [
            make(source(y_half[n]), target.at[n], y_dev[n], when=owns if n == 0 else ~owns)
            for n in range(3)
        ]

        @pl.when(owns)
        def _():
            copies[0].start()

        @pl.when(~owns)
        def _():
            copies[1].start()
            copies[2].start()

        return copies

    def first_sums(h, s, ra, owns):
        stack(h, s, 1)
        b = to_owners(lambda half: s.at[:, 1, rows32(half), :], rb, owns)
        stack(h, s, 0)
        a = {d: send(s.at[:, 0, rows16(x_peer[d]), :], ra.at[d], x_dev[d]) for d in (1, 0, 2)}
        return list(a.values()), b

    def second_sums(s, ra, pa, owns, copies):
        a, b = copies
        for copy in a:
            copy.wait_recv()
        for v in range(3):
            total = s[v, 0, rows16(xx), :].astype(jnp.float32)
            for d in range(3):
                total += ra[d, v].astype(jnp.float32)
            pa[v] = total.astype(jnp.bfloat16)
        a2 = to_owners(lambda half: pa, ra2, owns)
        b2 = [make(pb.at[:, :, cols256(x_peer[d])], rb2.at[d], x_dev[d], when=owns) for d in range(3)]

        @pl.when(owns)
        def _():
            for copy in b:
                copy.wait_recv()
            for v in range(3):
                total = s[v, 1, rows32(yhi), :].astype(jnp.float32)
                for d in range(3):
                    total += rb[d, v].astype(jnp.float32)
                pb[v] = total.astype(jnp.bfloat16)
            for copy in b2:
                copy.start()

        return a2, b2

    def finish(parts):
        linear = parts[0] * (1.0 / 4.0)
        phased = linear * jnp.sqrt(parts[1] * parts[1] + parts[2] * parts[2]) * (1.0 / 16.0)
        return linear.astype(jnp.bfloat16), phased.astype(jnp.bfloat16)

    piece_a = g.at[:, 0, rows16(xx), :]
    piece_b = g.at[:, 1, rows32(yhi), cols256(xx)]
    last_a = [make(piece_a, piece_a, dev) for dev in x_dev]
    last_b = [make(piece_b, piece_b, dev) for dev in g_dev]

    def results(pa, owns, copies):
        a2, b2 = copies

        @pl.when(owns)
        def _():
            for copy in a2:
                copy.wait_recv()
            parts = []
            for v in range(3):
                total = pa[v].astype(jnp.float32)
                for d in range(3):
                    total += ra2[d, v].astype(jnp.float32)
                parts.append(total)
            linear, phased = finish(parts)
            g[0, 0, rows16(xx), :] = linear
            g[1, 0, rows16(xx), :] = phased
            for copy in last_a:
                copy.start()
            for copy in b2:
                copy.wait_recv()
            parts = []
            for v in range(3):
                total = pb[v, :, cols256(xx)].astype(jnp.float32)
                for d in range(3):
                    total += rb2[d, v].astype(jnp.float32)
                parts.append(total)
            linear, phased = finish(parts)
            g[0, 1, rows32(yhi), cols256(xx)] = linear
            g[1, 1, rows32(yhi), cols256(xx)] = phased
            for copy in last_b:
                copy.start()

    pass_on = []
    for q in range(Q):
        mate_own[q].wait_recv()
        mate_far[q].wait_recv()
        for copy in forward[q]:
            copy.wait_recv()
        widen(q, 2, 8)
        for_early[q].wait_recv()
        pos = 10 - 9 * core
        pass_on.append(send(joined[q].at[pos], joined[q].at[pos], near(mate)))
        for_late[q].start()
        widen(q, 10 - 9 * core, 1)
        correlate(q, 0, early, owns_early)
    early_first = first_sums(0, s_early, ra_early, owns_early)
    for q in range(Q):
        pass_on[q].wait_recv()
        for_late[q].wait_recv()
        widen(q, 10 * core, 2)
        correlate(q, 1, late, owns_late)
    late_first = first_sums(1, s_late, ra_late, owns_late)
    early_second = second_sums(s_early, ra_early, pa_early, owns_early, early_first)
    late_second = second_sums(s_late, ra_late, pa_late, owns_late, late_first)
    results(pa_early, owns_early, early_second)
    results(pa_late, owns_late, late_second)

    bins_low = jnp.zeros((128, HALF_LAGS), jnp.float32)
    bins_high = jnp.zeros((128, HALF_LAGS), jnp.float32)
    for k in range(2):
        for copy in (last_a, last_b)[k]:
            copy.wait_recv()
        for out, v in ((lin_out, 0), (ph_out, 1)):
            low = jnp.dot(g[v, k, :, :HALF_LAGS], flip[...], preferred_element_type=jnp.float32)
            high = g[v, k, :, HALF_LAGS:]
            out[:, k, :HALF_LAGS] = low
            out[:, k, HALF_LAGS:] = high.astype(jnp.float32)
            if v == 0:
                column = member[k].astype(jnp.bfloat16)
                sides = (((0,), (0,)), ((), ()))
                bins_low += lax.dot_general(
                    column, low.astype(jnp.bfloat16), sides, preferred_element_type=jnp.float32)
                bins_high += lax.dot_general(column, high, sides, preferred_element_type=jnp.float32)
    bin_out[:, :HALF_LAGS] = bins_low[:NBIN]
    bin_out[:, HALF_LAGS:] = bins_high[:NBIN]
    for when, copy in sent:
        if when is None:
            copy.wait_send()
        else:
            pl.when(when)(copy.wait_send)


def stacks(wt, offs, keep, dist):
    vmem = pl.BlockSpec(memory_space=pltpu.VMEM)
    bf16, f32 = jnp.bfloat16, jnp.float32
    copies = 1 + 10 * Q + 2 * 12 + 10
    block = (12, 2, CH, KQ)
    return pl.pallas_call(
        kernel,
        out_shape=(
            jax.ShapeDtypeStruct((CH, 2, LAGS), f32),
            jax.ShapeDtypeStruct((CH, 2, LAGS), f32),
            jax.ShapeDtypeStruct((NBIN, LAGS), f32),
        ),
        in_specs=[pl.BlockSpec(memory_space=pl.ANY)] + [pl.BlockSpec(memory_space=pltpu.HBM)] * 3,
        out_specs=(vmem, vmem, vmem),
        scratch_shapes=[
            *[pltpu.VMEM(block, bf16)] * Q,
            pltpu.SMEM((1, 2), jnp.int32),
            pltpu.SMEM((2,), jnp.int32),
            pltpu.VMEM((1, 32 * CH), jnp.int32),
            pltpu.SMEM((1, 2), jnp.int32),
            pltpu.VMEM((Q * 2 * L, 12 * CH, 128), f32),
            pltpu.VMEM((2, CH, 128), f32),
            pltpu.VMEM((4, CH, 128), f32),
            pltpu.VMEM((2, CH, 128), f32),
            pltpu.VMEM((2, 8, F), f32),
            pltpu.VMEM((HALF_LAGS, HALF_LAGS), bf16),
            pltpu.VMEM((2, F // FINE, HALF_LAGS), f32),
            pltpu.VMEM((2, FINE, HALF_LAGS), f32),
            pltpu.VMEM((Q, KQ, LAGS), bf16),
            pltpu.VMEM((4 * CH, KQ), bf16),
            pltpu.VMEM((4 * CH, LAGS), f32),
            pltpu.VMEM((3, 2, CH, LAGS), bf16),
            pltpu.VMEM((3, 2, CH, LAGS), bf16),
            pltpu.VMEM((3, 3, 16, LAGS), bf16),
            pltpu.VMEM((3, 3, 16, LAGS), bf16),
            pltpu.VMEM((3, 16, LAGS), bf16),
            pltpu.VMEM((3, 16, LAGS), bf16),
            pltpu.VMEM((3, 3, 32, LAGS), bf16),
            pltpu.VMEM((3, 32, LAGS), bf16),
            pltpu.VMEM((3, 3, 16, LAGS), bf16),
            pltpu.VMEM((3, 3, 32, 256), bf16),
            pltpu.VMEM((2, 2, CH, LAGS), bf16),
            pltpu.SemaphoreType.DMA((Q,)),
            pltpu.SemaphoreType.DMA((3,)),
            pltpu.SemaphoreType.DMA((copies,)),
            pltpu.SemaphoreType.DMA((copies,)),
        ],
        compiler_params=pltpu.CompilerParams(
            collective_id=0, has_side_effects=True, vmem_limit_bytes=52 * 1024 * 1024
        ),
    )(wt, offs, keep, dist)


def local(spectra, band_offsets, window_keep, chan_dist):
    win_dev, ch_dev, _, freqs = spectra.shape
    wt = spectra.transpose(0, 2, 1, 3)
    linear, phased, binned = stacks(wt, band_offsets, window_keep, chan_dist[None, :])
    return linear, phased, binned


def solution(mesh):
    in_specs = (P("win", "chan", None, None), P("chan", None), P("win"), P())
    out_specs = (P("chan", None, None), P("chan", None, None), P("chan", None))
    return jax.shard_map(local, mesh=mesh, in_specs=in_specs, out_specs=out_specs, check_vma=False)
```
